512 devices in a mesh: gx: 64 (over z, x, core), gy: 8 (over y).
Axes of the slice: x: 4, y: 8, z: 8, core: 2. Of those that a mesh axis runs over, the one named last changes fastest.
Arguments:
- right_side: float32 [9, 1024, 4096], P(None, 'gx', 'gy'), may hold values from -6 to 6
- guess: float32 [9, 1024, 4096], P(None, 'gx', 'gy'), may hold values from -3 to 3
- vertical_coef: float32 [1024, 4096], P('gx', 'gy'), may hold values from 0.005 to 0.1
- breaking: int32 [1024, 4096], P('gx', 'gy'), may hold values 0 or 1
Outputs:
- updated: float32 [9, 1024, 4096], P(None, 'gx', 'gy')
- new_defect: float32 [9, 1024, 4096], P(None, 'gx', 'gy')
The draws below stay inside these ranges and needn't reach their ends.
All inputs are finite; a program needn't handle non-finite values. No bound on the sum of `breaking` on one device may be relied on, other than what follows from the above.
Results may differ from the reference program's by a relative error of at most 0.0003.
Values sent between devices are 32-bit elements; how exact they have to be, the bound alone decides.
No kernel may reach another device: no remote copies, remote signals or barrier semaphores. Data moves between devices by JAX's collectives and lax.ppermute only.
A program may use at most 128 MiB of HBM per device.

```python
import math
import jax
import jax.numpy as jnp
from jax import lax

K = 9
LEVELS = 5
PRE = 2
POST = 2
COARSE = 8
NX = 1024
NY = 4096


def set_ends(entries, rng, smallest, top_value):
    shape = entries.shape
    place = [jax.random.randint(jax.random.fold_in(rng, axis), (), 0, shape[axis]) for axis in range(len(shape))]
    entries = entries.at[tuple(place)].set(smallest)
    longest = shape.index(max(shape))
    place[longest] = (place[longest] + 1) % shape[longest]
    return entries.at[tuple(place)].set(top_value)


def levels(key, shape, cuts, smallest, top_value):
    factor_of = 1.0
    for position, shards_of in cuts:
        heights = jax.random.uniform(jax.random.fold_in(jax.random.fold_in(key, 6), position), (shards_of,), jnp.float32, smallest / len(cuts), top_value / len(cuts))
        factor_of = factor_of * jnp.repeat(jnp.exp(heights), shape[position] // shards_of).reshape((-1,) + (1,) * (len(shape) - 1 - position))
    return factor_of


def scatter_about(stream_key, dims, scale, reach, pieces=(), held_as=jnp.bfloat16):
    values = jax.random.normal(stream_key, dims, jnp.float32) * scale
    if len(pieces) > 0:
        values = levels(stream_key, dims, pieces, -0.22, 0.18) * values
    return jnp.clip(values, min=-reach, max=reach).astype(held_as)


def setup_inputs(seed: int = 0) -> dict:
    seeds = jax.random.split(jax.random.key(seed), 5)
    return {
        "right_side": scatter_about(seeds[0], (K, NX, NY), 1.0, 6.0, ((1, 64), (2, 8)), jnp.float32),
        "guess": scatter_about(seeds[1], (K, NX, NY), 0.5, 3.0, ((1, 64), (2, 8)), jnp.float32),
        "vertical_coef": jnp.clip(jnp.exp(math.log(0.1) - 2.9957323 * jax.random.uniform(seeds[2], (NX, NY), jnp.float32) ** levels(seeds[2], (NX, NY), ((0, 64), (1, 8)), -0.2, 0.2)), 0.005, 0.1),
        "breaking": set_ends((jax.random.randint(seeds[3], (NX, NY), 0, 4) < 1).astype(jnp.int32), jax.random.fold_in(seeds[3], 1), 0, 1),
    }


damping = 0.8
break_gain = 0.05


def coarsen(field):
    row_count, col_count = field.shape
    return field.reshape(row_count // 2, 2, col_count // 2, 2).mean(axis=(1, 3))


def fold_pairs(padded, axis):
    count = (padded.shape[axis] - 2) // 2

    def pick_rows(start):
        return lax.slice_in_dim(padded, start, start + 2 * count - 1, 2, axis)

    return (pick_rows(0) + 3.0 * pick_rows(1) + 3.0 * pick_rows(2) + pick_rows(3)) * 0.125


def prolong(coarse):
    depth, row_count, col_count = coarse.shape
    wide = jnp.broadcast_to(coarse[:, :, None, :, None], (depth, row_count, 2, col_count, 2))
    return wide.reshape(depth, 2 * row_count, 2 * col_count)


def local_apply(field, padded, vert_coef, center, scale):
    horizontal = padded[:, 2:, 1:-1] + padded[:, :-2, 1:-1] + padded[:, 1:-1, 2:] + padded[:, 1:-1, :-2]
    stacked = jnp.pad(field, ((1, 1), (0, 0), (0, 0)))
    vertical = stacked[2:] + stacked[:-2]
    return center * field - scale * horizontal - vert_coef * vertical


def reference(right_side, guess, vertical_coef, breaking):
    vert_list = [vertical_coef]
    break_list = [break_gain * breaking.astype(jnp.float32)]
    for level in range(1, LEVELS):
        vert_list.append(coarsen(vert_list[-1]))
        break_list.append(coarsen(break_list[-1]))
    center_list = [4.0 * 0.25 ** level + 2.0 * vert_list[level] + break_list[level] for level in range(LEVELS)]

    def operate(field, level):
        padded = jnp.pad(field, ((0, 0), (1, 1), (1, 1)))
        return local_apply(field, padded, vert_list[level], center_list[level], 0.25 ** level)

    def cycle(source, level):
        center = center_list[level]
        iterate = damping * source / center
        last = level == LEVELS - 1
        sweeps = COARSE if last else PRE
        for sweep in range(1, sweeps):
            iterate = iterate + damping * (source - operate(iterate, level)) / center
        if last:
            return iterate
        residual = source - operate(iterate, level)
        padded = jnp.pad(residual, ((0, 0), (1, 1), (1, 1)))
        coarse_source = fold_pairs(fold_pairs(padded, 1), 2)
        iterate = iterate + prolong(cycle(coarse_source, level + 1))
        for sweep in range(POST):
            iterate = iterate + damping * (source - operate(iterate, level)) / center
        return iterate

    defect = right_side - operate(guess, 0)
    updated = guess + cycle(defect, 0)
    new_defect = right_side - operate(updated, 0)
    return updated, new_defect
```

```python
import jax
import jax.numpy as jnp
from jax import lax
from jax.experimental import pallas as pl
from jax.experimental.pallas import tpu as pltpu
from jax.sharding import PartitionSpec as P

K = 9
PLANES = K + 2
VC, BT = K, K + 1
TILES = 23
SIDE = TILES // 2
damping = 0.8
keep = 0.2
break_gain = 0.05
F32 = jnp.float32
BF16 = jnp.bfloat16

COLS_AT = 24 * PLANES
TOP_AT = COLS_AT + 16
BOTTOM_AT = TOP_AT + 16
FAR_AT = BOTTOM_AT + 16
Y_ROWS = FAR_AT + 16


def lanes(rows):
    return lax.broadcasted_iota(jnp.int32, (rows, 128), 1)


def shifted(chunks):
    lane = lanes(chunks[0].shape[0])
    right = [pltpu.roll(v, 1, 1) for v in chunks]
    left = [pltpu.roll(v, 127, 1) for v in chunks]
    n = len(chunks)
    before = [jnp.where(lane == 0, right[c - 1], right[c]) if c else right[c] for c in range(n)]
    after = [jnp.where(lane == 127, left[c + 1], left[c]) if c < n - 1 else left[c] for c in range(n)]
    return before, after


def stencil(x, k, rows, at):
    count = x.shape[1]
    here = pl.ds(at, rows)
    v = [x[k + 1, c, here, :] for c in range(count)]
    before, after = shifted(v)
    out = []
    for c in range(count):
        hs = (x[k + 1, c, pl.ds(at - 1, rows), :] + x[k + 1, c, pl.ds(at + 1, rows), :]) + (before[c] + after[c])
        vs = x[k, c, here, :] + x[k + 2, c, here, :]
        out.append((v[c], hs, vs))
    return out


def each_plane(body, unrolled=False):
    if unrolled:
        for k in range(K):
            body(k)
    else:

        def step(k, carry):
            body(k)
            return carry

        lax.fori_loop(0, K, step, 0)


def clear_edges(x, rows):
    count, total = x.shape[1], x.shape[2]
    for k in (0, K + 1):
        x[k] = jnp.zeros((count, total, 128), F32)
    for k in range(1, K + 1):
        x[k, :, 0:8, :] = jnp.zeros((count, 8, 128), F32)
        x[k, :, 8 + rows : total, :] = jnp.zeros((count, total - 8 - rows, 128), F32)


def scales(f, inv, h):
    for c in range(f.shape[1]):
        vc = f[VC, c]
        center = 4.0 * h + 2.0 * vc + f[BT, c]
        inv[c] = jnp.where(vc > 0.0, damping / center, 0.0)


def first_sweep(x, f, inv, rows, unrolled=False):
    def body(k):
        for c in range(f.shape[1]):
            x[k + 1, c, pl.ds(8, rows), :] = inv[c] * f[k, c]

    each_plane(body, unrolled)


def sweep(x, y, f, inv, rows, h, unrolled=False):
    def body(k):
        for c, (v, hs, vs) in enumerate(stencil(x, k, rows, 8)):
            y[k + 1, c, pl.ds(8, rows), :] = keep * v + inv[c] * (f[k, c] + h * hs + f[VC, c] * vs)

    each_plane(body, unrolled)


def pair_matrix(inputs):
    i = lax.broadcasted_iota(jnp.int32, (inputs, 128), 0)
    j = lax.broadcasted_iota(jnp.int32, (inputs, 128), 1)
    return jnp.where((i == 2 * j) | (i == 2 * j + 1), 0.125, 0.0).astype(BF16)


def copy_matrix(outputs):
    i = lax.broadcasted_iota(jnp.int32, (128, outputs), 0)
    j = lax.broadcasted_iota(jnp.int32, (128, outputs), 1)
    return jnp.where((j == 2 * i) | (j == 2 * i + 1), 1.0, 0.0).astype(BF16)


def exact_dot(values, matrix):
    total = None
    for _ in range(3):
        part = values.astype(BF16)
        values = values - part.astype(F32)
        product = jnp.dot(part, matrix, preferred_element_type=F32)
        total = product if total is None else total + product
    return total


def restrict(x, f, rs, gs, rows, h, base, n, unrolled=False):
    count = f.shape[1]
    pairs = max(count // 2, 1)
    even = lanes(n) % 2 == 0
    rs[:, 0:8, :] = jnp.zeros((count, 8, 128), F32)
    rs[:, 8 + rows : 16 + rows, :] = jnp.zeros((count, 8, 128), F32)

    def put(k, c, value):
        at = pl.multiple_of((k * pairs + c // 2) * n, 8)
        gs[pl.ds(at, n), 128 * (c % 2) : 128 * (c % 2) + 128] = value

    def body(k):
        for c, (v, hs, vs) in enumerate(stencil(x, k, rows, 8)):
            vc = f[VC, c]
            center = 4.0 * h + 2.0 * vc + f[BT, c]
            rs[c, 8 : 8 + rows, :] = jnp.where(vc > 0.0, f[k, c] - center * v + h * hs + vc * vs, 0.0)
        folded = []
        for c in range(count):

            def pick(start):
                return rs[c, pl.ds(8 + base + start, n, stride=2), :]

            folded.append((pick(-1) + 3.0 * (pick(0) + pick(1)) + pick(2)) * 0.125)
        before, after = shifted(folded)
        for c in range(count):
            put(k, c, 3.0 * folded[c] + jnp.where(even, before[c], after[c]))

    each_plane(body, unrolled)
    for k in (VC, BT):
        for c in range(count):
            put(k, c, 2.0 * (f[k, c, pl.ds(base, n, stride=2), :] + f[k, c, pl.ds(base + 1, n, stride=2), :]))


def parity_copy(even, on, off, assemble):
    @pl.when(even)
    def _():
        assemble(off, on)

    @pl.when(jnp.logical_not(even))
    def _():
        assemble(on, off)


def pack_kernel(right_side, guess, vertical, breaking, f_out, to_left, to_right):
    shape = (16, 512)
    row = lax.broadcasted_iota(jnp.int32, shape, 0)
    col = lax.broadcasted_iota(jnp.int32, shape, 1)
    lane = lanes(16)
    lane8 = lanes(8)
    vc = vertical[...]
    bt = break_gain * breaking[...].astype(F32)
    center = 4.0 + 2.0 * vc + bt

    def pack(plane, field):
        near, far = field[:, 0:128], field[:, 128:256]
        to_left[24 * plane : 24 * plane + 16, :] = near
        to_left[24 * plane + 16 : 24 * plane + 24, :] = jnp.where(
            lane8 < 64, far[0:8], pltpu.roll(far[8:16], 64, 1)
        )
        near, far = field[:, 384:512], field[:, 256:384]
        to_right[24 * plane : 24 * plane + 16, :] = near
        to_right[24 * plane + 16 : 24 * plane + 24, :] = jnp.where(
            lane8 >= 64, far[0:8], pltpu.roll(far[8:16], 64, 1)
        )

    first = jnp.zeros((16, 128), F32)
    last = jnp.zeros((16, 128), F32)
    to_left[TOP_AT:Y_ROWS, :] = jnp.zeros((Y_ROWS - TOP_AT, 128), F32)
    to_right[TOP_AT:Y_ROWS, :] = jnp.zeros((Y_ROWS - TOP_AT, 128), F32)
    lane1 = lanes(1)
    for k in range(K):
        v = guess[k]
        hs = jnp.where(row > 0, pltpu.roll(v, 1, 0), 0.0) + jnp.where(row < 15, pltpu.roll(v, 15, 0), 0.0)
        hs = hs + jnp.where(col > 0, pltpu.roll(v, 1, 1), 0.0) + jnp.where(col < 511, pltpu.roll(v, 511, 1), 0.0)
        f = right_side[k] - center * v + hs
        if k == 0:
            f = f + vc * guess[1]
        elif k == K - 1:
            f = f + vc * guess[K - 2]
        else:
            f = f + vc * (guess[k - 1] + guess[k + 1])
        for c in range(4):
            f_out[k, c] = f[:, 128 * c : 128 * c + 128]
        pack(k, f)
        first = jnp.where(lane == k, jnp.broadcast_to(v[:, 0:1], (16, 128)), first)
        last = jnp.where(lane == k, jnp.broadcast_to(v[:, 511:512], (16, 128)), last)
        top, bottom = v[0:1], v[15:16]
        to_left[TOP_AT + k : TOP_AT + k + 1, :] = top[:, 0:128]
        to_left[BOTTOM_AT + k : BOTTOM_AT + k + 1, :] = bottom[:, 0:128]
        to_left[FAR_AT + k : FAR_AT + k + 1, :] = jnp.where(
            lane1 < 64, top[:, 128:256], pltpu.roll(bottom[:, 128:256], 64, 1)
        )
        to_right[TOP_AT + k : TOP_AT + k + 1, :] = top[:, 384:512]
        to_right[BOTTOM_AT + k : BOTTOM_AT + k + 1, :] = bottom[:, 384:512]
        to_right[FAR_AT + k : FAR_AT + k + 1, :] = jnp.where(
            lane1 >= 64, top[:, 256:384], pltpu.roll(bottom[:, 256:384], 64, 1)
        )
    pack(VC, vc)
    pack(BT, bt)
    to_left[COLS_AT : COLS_AT + 16, :] = first
    to_right[COLS_AT : COLS_AT + 16, :] = last


def widen_kernel(f_own, guess, vertical, breaking, from_left, from_right, q):
    lane = lanes(16)
    lane8 = lanes(8)
    lane1 = lanes(1)
    left_cols = from_left[COLS_AT : COLS_AT + 16, :]
    right_cols = from_right[COLS_AT : COLS_AT + 16, :]
    for k in range(PLANES):
        far = from_left[24 * k + 16 : 24 * k + 24, :]
        q[k, 0, 0:8, :] = jnp.where(lane8 >= 64, far, 0.0)
        q[k, 0, 8:16, :] = jnp.where(lane8 >= 64, pltpu.roll(far, 64, 1), 0.0)
        far = from_right[24 * k + 16 : 24 * k + 24, :]
        q[k, 7, 0:8, :] = jnp.where(lane8 < 64, far, 0.0)
        q[k, 7, 8:16, :] = jnp.where(lane8 < 64, pltpu.roll(far, 64, 1), 0.0)
        near_left = from_left[24 * k : 24 * k + 16, :]
        near_right = from_right[24 * k : 24 * k + 16, :]
        if k < K:
            v = guess[k]
            first = jnp.broadcast_to(v[:, 0:1], (16, 128))
            last = jnp.broadcast_to(v[:, 511:512], (16, 128))
            q[k, 1] = near_left + jnp.where(lane == 127, first, 0.0)
            q[k, 6] = near_right + jnp.where(lane == 0, last, 0.0)
            left = jnp.broadcast_to(left_cols[:, k : k + 1], (16, 128))
            right = jnp.broadcast_to(right_cols[:, k : k + 1], (16, 128))
            q[k, 2] = f_own[k, 0] + jnp.where(lane == 0, left, 0.0)
            q[k, 3] = f_own[k, 1]
            q[k, 4] = f_own[k, 2]
            q[k, 5] = f_own[k, 3] + jnp.where(lane == 127, right, 0.0)
        else:
            q[k, 1] = near_left
            q[k, 6] = near_right
            own = vertical[...] if k == VC else break_gain * breaking[...].astype(F32)
            for c in range(4):
                q[k, 2 + c] = own[:, 128 * c : 128 * c + 128]
    for plane, row, near_at in ((PLANES, 0, TOP_AT), (PLANES + 1, 15, BOTTOM_AT)):
        for c in range(8):
            q[plane, c] = jnp.zeros((16, 128), F32)
        for k in range(K):
            at = slice(k, k + 1)
            v = guess[k, row : row + 1, :]
            for c in range(4):
                q[plane, 2 + c, at, :] = v[:, 128 * c : 128 * c + 128]
            q[plane, 1, at, :] = from_left[near_at + k : near_at + k + 1, :]
            q[plane, 6, at, :] = from_right[near_at + k : near_at + k + 1, :]
            far_left = from_left[FAR_AT + k : FAR_AT + k + 1, :]
            far_right = from_right[FAR_AT + k : FAR_AT + k + 1, :]
            if plane == PLANES + 1:
                far_left = pltpu.roll(far_left, 64, 1)
                far_right = pltpu.roll(far_right, 64, 1)
            q[plane, 0, at, :] = jnp.where(lane1 >= 64, far_left, 0.0)
            q[plane, 7, at, :] = jnp.where(lane1 < 64, far_right, 0.0)


def fine_kernel(q, on, off, x0_out, f0_out, x1_out, f1_out, f2_out, f, xa, xb, inv, rs, gs, f1, xc, xd, inv1, rs1, gs1):
    even = lax.axis_index("gx") % 2 == 0

    def assemble(up, down):
        for k in range(PLANES):
            f[k, :, 0:16, :] = up[k]
            f[k, :, 16:32, :] = q[k]
            f[k, :, 32:48, :] = down[k]
        for k in range(K):
            row = slice(k, k + 1)
            f[k, :, 15:16, :] += q[PLANES, :, row, :]
            f[k, :, 16:17, :] += up[PLANES + 1, :, row, :]
            f[k, :, 31:32, :] += down[PLANES, :, row, :]
            f[k, :, 32:33, :] += q[PLANES + 1, :, row, :]

    parity_copy(even, on, off, assemble)
    clear_edges(xa, 48)
    clear_edges(xb, 48)
    scales(f, inv, 1.0)
    first_sweep(xa, f, inv, 48)
    sweep(xa, xb, f, inv, 48, 1.0)
    restrict(xb, f, rs, gs, 48, 1.0, 0, 24)
    for k in range(K):
        x0_out[k] = xb[k + 1, 1:7, 20:44, :]
    for k in range(PLANES):
        f0_out[k] = f[k, 1:7, 12:36, :]
    pairs = exact_dot(gs[...], pair_matrix(256))
    for k in range(PLANES):
        for c in range(4):
            at = (4 * k + c) * 24
            f1[k, c] = pairs[at : at + 24]

    clear_edges(xc, 24)
    clear_edges(xd, 24)
    scales(f1, inv1, 0.25)
    first_sweep(xc, f1, inv1, 24)
    sweep(xc, xd, f1, inv1, 24, 0.25)
    restrict(xd, f1, rs1, gs1, 24, 0.25, 4, 8)
    for k in range(K):
        x1_out[k] = xd[k + 1, :, 12:28, :]
    for k in range(PLANES):
        f1_out[k] = f1[k, :, 4:20, :]
    pairs = exact_dot(gs1[...], pair_matrix(256))
    for k in range(PLANES):
        for c in range(2):
            at = (2 * k + c) * 8
            f2_out[k, c] = pairs[at : at + 8]


def middle_kernel(own, on, off, x2_out, f2, chunk, xa, xb, inv, rs, gs):
    even = lax.axis_index("gx") % 2 == 0

    def assemble(up, down):
        for k in range(PLANES):
            f2[k, :, 0:1, :] = jnp.zeros((2, 1, 128), F32)
            f2[k, :, 1:6, :] = up[k, :, 1:6, :]
            f2[k, :, 6:10, :] = own[k, :, 2:6, :]
            f2[k, :, 10:15, :] = down[k, :, 2:7, :]
            f2[k, :, 15:16, :] = jnp.zeros((2, 1, 128), F32)

    parity_copy(even, on, off, assemble)
    h = 0.25**2
    clear_edges(xa, 16)
    clear_edges(xb, 16)
    scales(f2, inv, h)
    first_sweep(xa, f2, inv, 16, True)
    sweep(xa, xb, f2, inv, 16, h, True)
    restrict(xb, f2, rs, gs, 16, h, 0, 8, True)
    for k in range(K):
        x2_out[k] = xb[k + 1, :, 8:24, :]
    pairs = exact_dot(gs[...], pair_matrix(256))
    rows = [pairs[8 * k + 3 : 8 * k + 5] for k in range(PLANES)]
    rows.append(jnp.zeros((2, 128), F32))
    piece = jnp.concatenate(rows, axis=0)

    def fill(i, carry):
        chunk[i] = piece
        return carry

    lax.fori_loop(0, chunk.shape[0], fill, 0)


def add_copies(x, coarse, es, at_row, n, rows, first, count):
    chunks = coarse.shape[1]
    for k in range(K):
        for c in range(chunks):
            es[(k * chunks + c) * n : (k * chunks + c) * n + n, :] = coarse[k + 1, c, 8 + at_row : 8 + at_row + n, :]
    wide = exact_dot(es[...], copy_matrix(256))
    skip = (2 * n - rows) // 4
    used = rows // 2
    for k in range(K):
        for c in range(chunks):
            base = (k * chunks + c) * n + skip
            for half in range(2):
                fc = 2 * c + half - first
                if 0 <= fc < count:
                    e = wide[base : base + used, 128 * half : 128 * half + 128]
                    for p in range(2):
                        x[k + 1, fc, pl.ds(8 + p, used, stride=2), :] += e


def coarse_kernel(
    same, other, x2_in, f2, x1_in, f1, x0_in, f0, guess, updated, new_defect,
    f3, xa, xb, inv3, rs3, gs3, f4, ya, yb, inv4, es2, xc, xd, inv2, es1, xe, xf, inv1, es0, xg, xh, inv0,
):
    gx = lax.axis_index("gx")
    tiles = 2 * same.shape[0]
    for t in range(TILES):
        tile = gx - SIDE + t
        valid = jnp.logical_and(tile >= 0, tile < tiles)
        chip = jnp.clip(tile, 0, tiles - 1) // 2
        piece = jnp.where(valid, (same if t % 2 else other)[chip], 0.0)
        for k in range(PLANES):
            f3[k, 0, 2 * t : 2 * t + 2, :] = piece[2 * k : 2 * k + 2]
    for k in range(PLANES):
        f3[k, 0, 2 * TILES : 48, :] = jnp.zeros((48 - 2 * TILES, 128), F32)
    h = 0.25**3
    clear_edges(xa, 48)
    clear_edges(xb, 48)
    scales(f3, inv3, h)
    first_sweep(xa, f3, inv3, 48, True)
    sweep(xa, xb, f3, inv3, 48, h, True)
    restrict(xb, f3, rs3, gs3, 48, h, 0, 24, True)
    pairs = exact_dot(gs3[...], pair_matrix(128))
    for k in range(PLANES):
        f4[k, 0] = pairs[24 * k : 24 * k + 24]

    h = 0.25**4
    clear_edges(ya, 24)
    clear_edges(yb, 24)
    scales(f4, inv4, h)
    first_sweep(ya, f4, inv4, 24, True)
    for _ in range(3):
        sweep(ya, yb, f4, inv4, 24, h, True)
        sweep(yb, ya, f4, inv4, 24, h, True)
    sweep(ya, yb, f4, inv4, 24, h, True)

    h = 0.25**3
    for k in range(K):
        wide = exact_dot(yb[k + 1, 0, 8:32, :], copy_matrix(128))
        for p in range(2):
            xb[k + 1, 0, pl.ds(8 + p, 24, stride=2), :] += wide
    sweep(xb, xa, f3, inv3, 48, h, True)
    sweep(xa, xb, f3, inv3, 48, h, True)

    h = 0.25**2
    clear_edges(xc, 16)
    clear_edges(xd, 16)
    scales(f2, inv2, h)
    for k in range(K):
        xc[k + 1, :, 8:24, :] = x2_in[k]
    add_copies(xc, xb, es2, 19, 8, 16, 0, 2)
    sweep(xc, xd, f2, inv2, 16, h, True)
    sweep(xd, xc, f2, inv2, 16, h, True)

    h = 0.25
    clear_edges(xe, 16)
    clear_edges(xf, 16)
    scales(f1, inv1, h)
    for k in range(K):
        xe[k + 1, :, 8:24, :] = x1_in[k]
    add_copies(xe, xc, es1, 4, 8, 16, 0, 4)
    sweep(xe, xf, f1, inv1, 16, h)
    sweep(xf, xe, f1, inv1, 16, h)

    clear_edges(xg, 24)
    clear_edges(xh, 24)
    scales(f0, inv0, 1.0)
    for k in range(K):
        xg[k + 1, :, 8:32, :] = x0_in[k]
    add_copies(xg, xe, es0, 0, 16, 24, 1, 6)
    sweep(xg, xh, f0, inv0, 24, 1.0)
    sweep(xh, xg, f0, inv0, 24, 1.0)

    def finish(k):
        for c, (v, hs, vs) in enumerate(stencil(xg, k, 16, 12)):
            if 1 <= c <= 4:
                vc = f0[VC, c, 4:20, :]
                center = 4.0 + 2.0 * vc + f0[BT, c, 4:20, :]
                cols = slice(128 * (c - 1), 128 * c)
                new_defect[k, :, cols] = f0[k, c, 4:20, :] - center * v + hs + vc * vs
                updated[k, :, cols] = guess[k, :, cols] + v

    each_plane(finish)


def call(kernel, name, outs, scratch, *operands):
    spec = pl.BlockSpec(memory_space=pltpu.VMEM)
    return pl.pallas_call(
        kernel,
        name=name,
        out_shape=[jax.ShapeDtypeStruct(s, F32) for s in outs],
        in_specs=[spec] * len(operands),
        out_specs=[spec] * len(outs),
        scratch_shapes=[pltpu.VMEM(s, F32) for s in scratch],
        compiler_params=pltpu.CompilerParams(vmem_limit_bytes=48 * 1024 * 1024),
    )(*operands)


def field(chunks, rows):
    return (K + 2, chunks, rows + 16, 128)


def shards(right_side, guess, vertical, breaking):
    nx, ny = lax.axis_size("gx"), lax.axis_size("gy")
    chip = [(i, i ^ 1) for i in range(nx)]
    gap = [(i, i + 1) for i in range(1, nx - 1, 2)]
    gap = gap + [(b, a) for a, b in gap]
    rows = [(16, 512)]

    f_own, to_left, to_right = call(
        pack_kernel, "pack", [(K, 4, 16, 128), (Y_ROWS, 128), (Y_ROWS, 128)], [], right_side, guess, vertical, breaking
    )
    from_right = lax.ppermute(to_left, "gy", [(j + 1, j) for j in range(ny - 1)])
    from_left = lax.ppermute(to_right, "gy", [(j, j + 1) for j in range(ny - 1)])
    (q,) = call(widen_kernel, "widen", [(PLANES + 2, 8, 16, 128)], [], f_own, guess, vertical, breaking, from_left, from_right)
    off = lax.ppermute(q, "gx", gap)
    on = lax.ppermute(q, "gx", chip)
    x0, f0, x1, f1, f2_own = call(
        fine_kernel,
        "fine",
        [(K, 6, 24, 128), (PLANES, 6, 24, 128), (K, 4, 16, 128), (PLANES, 4, 16, 128), (PLANES, 2, 8, 128)],
        [
            (PLANES, 8, 48, 128), field(8, 48), field(8, 48), (8, 48, 128), (8, 64, 128), (PLANES * 4 * 24, 256),
            (PLANES, 4, 24, 128), field(4, 24), field(4, 24), (4, 24, 128), (4, 40, 128), (PLANES * 2 * 8, 256),
        ],
        q, on, off,
    )
    off = lax.ppermute(f2_own, "gx", gap)
    on = lax.ppermute(f2_own, "gx", chip)
    x2, f2, chunk = call(
        middle_kernel,
        "middle",
        [(K, 2, 16, 128), (PLANES, 2, 16, 128), (nx // 2, 24, 128)],
        [field(2, 16), field(2, 16), (2, 16, 128), (2, 32, 128), (PLANES * 8, 256)],
        f2_own, on, off,
    )
    same = lax.all_to_all(
        chunk, "gx", 0, 0, axis_index_groups=[list(range(0, nx, 2)), list(range(1, nx, 2))], tiled=True
    )
    other = lax.ppermute(same, "gx", chip)
    return tuple(
        call(
            coarse_kernel,
            "coarse",
            [(K, 16, 512), (K, 16, 512)],
            [
                (PLANES, 1, 48, 128), field(1, 48), field(1, 48), (1, 48, 128), (1, 64, 128), (PLANES * 24, 128),
                (PLANES, 1, 24, 128), field(1, 24), field(1, 24), (1, 24, 128),
                (K * 8, 128), field(2, 16), field(2, 16), (2, 16, 128),
                (K * 2 * 8, 128), field(4, 16), field(4, 16), (4, 16, 128),
                (K * 4 * 16, 128), field(6, 24), field(6, 24), (6, 24, 128),
            ],
            same, other, x2, f2, x1, f1, x0, f0, guess,
        )
    )


def solution(mesh):
    in_specs = (P(None, "gx", "gy"), P(None, "gx", "gy"), P("gx", "gy"), P("gx", "gy"))
    out_specs = (P(None, "gx", "gy"), P(None, "gx", "gy"))
    return jax.shard_map(shards, mesh=mesh, in_specs=in_specs, out_specs=out_specs, check_vma=False)
```

```python
import jax
import jax.numpy as jnp
from jax import lax
from jax.experimental import pallas as pl
from jax.experimental.pallas import tpu as pltpu
from jax.sharding import PartitionSpec as P

K = 9
PLANES = K + 2
VC, BT = K, K + 1
TILES = 23
SIDE = TILES // 2
damping = 0.8
keep = 0.2
break_gain = 0.05
F32 = jnp.float32
BF16 = jnp.bfloat16

COLS_AT = 24 * PLANES
TOP_AT = COLS_AT + 16
BOTTOM_AT = TOP_AT + 16
FAR_AT = BOTTOM_AT + 16
Y_ROWS = FAR_AT + 16

SHORT_AT = 8 * PLANES
GUESS_AT = SHORT_AT + 5 * PLANES
X_ROWS = GUESS_AT + K


def lanes(rows):
    return lax.broadcasted_iota(jnp.int32, (rows, 128), 1)


def shifted(chunks):
    lane = lanes(chunks[0].shape[0])
    right = [pltpu.roll(v, 1, 1) for v in chunks]
    left = [pltpu.roll(v, 127, 1) for v in chunks]
    n = len(chunks)
    before = [jnp.where(lane == 0, right[c - 1], right[c]) if c else right[c] for c in range(n)]
    after = [jnp.where(lane == 127, left[c + 1], left[c]) if c < n - 1 else left[c] for c in range(n)]
    return before, after


def stencil(x, k, rows, at):
    count = x.shape[1]
    here = pl.ds(at, rows)
    v = [x[k + 1, c, here, :] for c in range(count)]
    before, after = shifted(v)
    out = []
    for c in range(count):
        hs = (x[k + 1, c, pl.ds(at - 1, rows), :] + x[k + 1, c, pl.ds(at + 1, rows), :]) + (before[c] + after[c])
        vs = x[k, c, here, :] + x[k + 2, c, here, :]
        out.append((v[c], hs, vs))
    return out


def clear_edges(x, rows):
    count, total = x.shape[1], x.shape[2]
    for k in (0, K + 1):
        x[k] = jnp.zeros((count, total, 128), F32)
    for k in range(1, K + 1):
        x[k, :, 0:8, :] = jnp.zeros((count, 8, 128), F32)
        x[k, :, 8 + rows : total, :] = jnp.zeros((count, total - 8 - rows, 128), F32)


def scales(f, inv, ratio, h):
    for c in range(f.shape[1]):
        vc = f[VC, c]
        center = 4.0 * h + 2.0 * vc + f[BT, c]
        inv[c] = jnp.where(vc > 0.0, damping / center, 0.0)
        if ratio is not None:
            ratio[c] = center * (1.0 / damping)


def first_sweep(x, f, inv, rows):
    for k in range(K):
        for c in range(f.shape[1]):
            x[k + 1, c, pl.ds(8, rows), :] = inv[c] * f[k, c]


def times(h, value):
    return value if h == 1.0 else h * value


def second_sweep(x, y, f, inv, rows, h):
    for k in range(K):
        for c, (v, hs, vs) in enumerate(stencil(x, k, rows, 8)):
            y[k + 1, c, pl.ds(8, rows), :] = (1.0 + keep) * v + inv[c] * (times(h, hs) + f[VC, c] * vs)


def sweep(x, y, f, inv, rows, h):
    for k in range(K):
        for c, (v, hs, vs) in enumerate(stencil(x, k, rows, 8)):
            y[k + 1, c, pl.ds(8, rows), :] = keep * v + inv[c] * (f[k, c] + times(h, hs) + f[VC, c] * vs)


def pair_matrix(inputs):
    i = lax.broadcasted_iota(jnp.int32, (inputs, 128), 0)
    j = lax.broadcasted_iota(jnp.int32, (inputs, 128), 1)
    return jnp.where((i == 2 * j) | (i == 2 * j + 1), 0.25, 0.0).astype(BF16)


def fold_matrix(inputs):
    i = lax.broadcasted_iota(jnp.int32, (inputs, 128), 0)
    d = i - 2 * lax.broadcasted_iota(jnp.int32, (inputs, 128), 1)
    inner = jnp.where((d == 0) | (d == 1), 0.375, 0.0)
    return jnp.where((d == -1) | (d == 2), 0.125, inner).astype(BF16)


def copy_matrix(outputs):
    i = lax.broadcasted_iota(jnp.int32, (128, outputs), 0)
    j = lax.broadcasted_iota(jnp.int32, (128, outputs), 1)
    return jnp.where((j == 2 * i) | (j == 2 * i + 1), 1.0, 0.0).astype(BF16)


def exact_dot(values, matrix, parts=3):
    total = None
    for _ in range(parts):
        part = values.astype(BF16)
        values = values - part.astype(F32)
        product = jnp.dot(part, matrix, preferred_element_type=F32)
        total = product if total is None else total + product
    return total


def restrict(x, f, inv, ratio, rs, gs, coarse, rows, h, base, n):
    count = f.shape[1]
    pairs = max(count // 2, 1)
    width = gs.shape[-1]
    lane = lanes(n)
    rs[:, 0:8, :] = jnp.zeros((count, 8, 128), F32)
    rs[:, 8 + rows : 16 + rows, :] = jnp.zeros((count, 8, 128), F32)

    def part(slot, c):
        return gs[slot, (c // 2) * n : (c // 2) * n + n, 128 * (c % 2) : 128 * (c % 2) + 128]

    def put(slot, c, value):
        gs[slot, (c // 2) * n : (c // 2) * n + n, 128 * (c % 2) : 128 * (c % 2) + 128] = value

    def residual(k, slot):
        for c, (v, hs, vs) in enumerate(stencil(x, k, rows, 8)):
            around = inv[c] * (f[k, c] + times(h, hs) + f[VC, c] * vs)
            rs[c, 8 : 8 + rows, :] = ratio[c] * (around - damping * v)
        for c in range(count):

            def pick(start):
                return rs[c, pl.ds(8 + base + start, n, stride=2), :]

            put(slot, c, (pick(-1) + 3.0 * (pick(0) + pick(1)) + pick(2)) * 0.125)

    def emit(k, slot, values):
        for j in range(pairs):
            value = values[j * n : j * n + n]
            if j > 0:
                value = value + jnp.where(lane == 0, 0.125 * pltpu.roll(part(slot, 2 * j - 1), 1, 1), 0.0)
            if j < pairs - 1:
                value = value + jnp.where(lane == 127, 0.125 * pltpu.roll(part(slot, 2 * j + 2), 127, 1), 0.0)
            coarse[k, j] = value

    matrix = fold_matrix(width)
    for k in range(K):
        residual(k, k)
    size = pairs * n
    values = exact_dot(gs[...].reshape(K * size, width), matrix, 2)
    for k in range(K):
        emit(k, k, values[k * size : k * size + size])
    for slot, k in enumerate((VC, BT)):
        for c in range(count):
            put(slot, c, f[k, c, pl.ds(base, n, stride=2), :] + f[k, c, pl.ds(base + 1, n, stride=2), :])
    values = exact_dot(gs[0:2].reshape(2 * pairs * n, width), pair_matrix(width))
    for slot, k in enumerate((VC, BT)):
        for j in range(pairs):
            at = (slot * pairs + j) * n
            coarse[k, j] = values[at : at + n]


def parity_copy(even, on, off, assemble):
    @pl.when(even)
    def _():
        assemble(off, on)

    @pl.when(jnp.logical_not(even))
    def _():
        assemble(on, off)


def own_defect(right_side, guess, vc, bt, k, left, right):
    v = guess[k]
    row = lax.broadcasted_iota(jnp.int32, v.shape, 0)
    col = lax.broadcasted_iota(jnp.int32, v.shape, 1)
    hs = jnp.where(row > 0, pltpu.roll(v, 1, 0), 0.0) + jnp.where(row < 15, pltpu.roll(v, 15, 0), 0.0)
    hs = hs + jnp.where(col > 0, pltpu.roll(v, 1, 1), left) + jnp.where(col < 511, pltpu.roll(v, 511, 1), right)
    vs = guess[1] if k == 0 else guess[K - 2] if k == K - 1 else guess[k - 1] + guess[k + 1]
    return right_side[k] - (4.0 + 2.0 * vc + bt) * v + hs + vc * vs


def pack_kernel(rs_in, g_in, vc_in, br_in, to_left, to_right, right_side, guess, vertical, breaking, sems):
    pairs = ((vc_in, vertical), (br_in, breaking), (g_in, guess), (rs_in, right_side))
    copies = [pltpu.make_async_copy(a, b, sems.at[i]) for i, (a, b) in enumerate(pairs)]
    for copy in copies:
        copy.start()
    for copy in copies:
        copy.wait()
    lane = lanes(16)
    lane8 = lanes(8)
    vc = vertical[...]
    bt = break_gain * breaking[...].astype(F32)

    def pack(plane, field):
        near, far = field[:, 0:128], field[:, 128:256]
        to_left[24 * plane : 24 * plane + 16, :] = near
        to_left[24 * plane + 16 : 24 * plane + 24, :] = jnp.where(
            lane8 < 64, far[0:8], pltpu.roll(far[8:16], 64, 1)
        )
        near, far = field[:, 384:512], field[:, 256:384]
        to_right[24 * plane : 24 * plane + 16, :] = near
        to_right[24 * plane + 16 : 24 * plane + 24, :] = jnp.where(
            lane8 >= 64, far[0:8], pltpu.roll(far[8:16], 64, 1)
        )

    first = jnp.zeros((16, 128), F32)
    last = jnp.zeros((16, 128), F32)
    to_left[TOP_AT:Y_ROWS, :] = jnp.zeros((Y_ROWS - TOP_AT, 128), F32)
    to_right[TOP_AT:Y_ROWS, :] = jnp.zeros((Y_ROWS - TOP_AT, 128), F32)
    lane1 = lanes(1)
    for k in range(K):
        v = guess[k]
        f = own_defect(right_side, guess, vc, bt, k, 0.0, 0.0)
        pack(k, f)
        first = jnp.where(lane == k, jnp.broadcast_to(v[:, 0:1], (16, 128)), first)
        last = jnp.where(lane == k, jnp.broadcast_to(v[:, 511:512], (16, 128)), last)
        top, bottom = v[0:1], v[15:16]
        to_left[TOP_AT + k : TOP_AT + k + 1, :] = top[:, 0:128]
        to_left[BOTTOM_AT + k : BOTTOM_AT + k + 1, :] = bottom[:, 0:128]
        to_left[FAR_AT + k : FAR_AT + k + 1, :] = jnp.where(
            lane1 < 64, top[:, 128:256], pltpu.roll(bottom[:, 128:256], 64, 1)
        )
        to_right[TOP_AT + k : TOP_AT + k + 1, :] = top[:, 384:512]
        to_right[BOTTOM_AT + k : BOTTOM_AT + k + 1, :] = bottom[:, 384:512]
        to_right[FAR_AT + k : FAR_AT + k + 1, :] = jnp.where(
            lane1 >= 64, top[:, 256:384], pltpu.roll(bottom[:, 256:384], 64, 1)
        )
    pack(VC, vc)
    pack(BT, bt)
    to_left[COLS_AT : COLS_AT + 16, :] = first
    to_right[COLS_AT : COLS_AT + 16, :] = last


def widen_kernel(right_side, guess, vertical, breaking, from_left, from_right, q, to_on, to_off):
    lane = lanes(16)
    lane8 = lanes(8)
    lane1 = lanes(1)
    left_cols = from_left[COLS_AT : COLS_AT + 16, :]
    right_cols = from_right[COLS_AT : COLS_AT + 16, :]
    vc = vertical[...]
    bt = break_gain * breaking[...].astype(F32)
    for k in range(PLANES):
        far = from_left[24 * k + 16 : 24 * k + 24, :]
        q[k, 0, 0:8, :] = jnp.where(lane8 >= 64, far, 0.0)
        q[k, 0, 8:16, :] = jnp.where(lane8 >= 64, pltpu.roll(far, 64, 1), 0.0)
        far = from_right[24 * k + 16 : 24 * k + 24, :]
        q[k, 7, 0:8, :] = jnp.where(lane8 < 64, far, 0.0)
        q[k, 7, 8:16, :] = jnp.where(lane8 < 64, pltpu.roll(far, 64, 1), 0.0)
        near_left = from_left[24 * k : 24 * k + 16, :]
        near_right = from_right[24 * k : 24 * k + 16, :]
        if k < K:
            v = guess[k]
            first = jnp.broadcast_to(v[:, 0:1], (16, 128))
            last = jnp.broadcast_to(v[:, 511:512], (16, 128))
            q[k, 1] = near_left + jnp.where(lane == 127, first, 0.0)
            q[k, 6] = near_right + jnp.where(lane == 0, last, 0.0)
            own = own_defect(right_side, guess, vc, bt, k, left_cols[:, k : k + 1], right_cols[:, k : k + 1])
        else:
            q[k, 1] = near_left
            q[k, 6] = near_right
            own = vc if k == VC else bt
        for c in range(4):
            q[k, 2 + c] = own[:, 128 * c : 128 * c + 128]
    for plane, row, near_at in ((PLANES, 0, TOP_AT), (PLANES + 1, 15, BOTTOM_AT)):
        for c in range(8):
            q[plane, c] = jnp.zeros((16, 128), F32)
        for k in range(K):
            at = slice(k, k + 1)
            v = guess[k, row : row + 1, :]
            for c in range(4):
                q[plane, 2 + c, at, :] = v[:, 128 * c : 128 * c + 128]
            q[plane, 1, at, :] = from_left[near_at + k : near_at + k + 1, :]
            q[plane, 6, at, :] = from_right[near_at + k : near_at + k + 1, :]
            far_left = from_left[FAR_AT + k : FAR_AT + k + 1, :]
            far_right = from_right[FAR_AT + k : FAR_AT + k + 1, :]
            if plane == PLANES + 1:
                far_left = pltpu.roll(far_left, 64, 1)
                far_right = pltpu.roll(far_right, 64, 1)
            q[plane, 0, at, :] = jnp.where(lane1 >= 64, far_left, 0.0)
            q[plane, 7, at, :] = jnp.where(lane1 < 64, far_right, 0.0)


    def fill(buffer, long, short, plane):
        for c in range(7):
            for k in range(PLANES):
                piece = jnp.where(lane < 64, q[k, 7], q[k, 0]) if c == 0 else q[k, c]
                buffer[c, 8 * k : 8 * k + 8, :] = piece[long : long + 8]
                buffer[c, SHORT_AT + 5 * k : SHORT_AT + 5 * k + 5, :] = piece[short : short + 5]
            piece = jnp.where(lane < 64, q[plane, 7], q[plane, 0]) if c == 0 else q[plane, c]
            buffer[c, GUESS_AT : GUESS_AT + K, :] = piece[0:K]

    def fill_both(to_up, to_down):
        fill(to_up, 0, 8, PLANES)
        fill(to_down, 8, 3, PLANES + 1)

    parity_copy(lax.axis_index("gx") % 2 == 0, to_on, to_off, fill_both)


def fine_kernel(q, off, on, x0_out, f0_out, x1_out, f1_out, f2_out, f, xa, xb, inv, ratio, rs, gs, f1, xc, xd, inv1, ratio1, rs1, gs1):
    even = lax.axis_index("gx") % 2 == 0

    def assemble(up, down):
        lane = lanes(8)

        def piece(buffer, c, at, n):
            value = buffer[min(c % 7, c), at : at + n, :]
            if c == 0:
                return jnp.where(lane[0:n] >= 64, value, 0.0)
            return jnp.where(lane[0:n] < 64, value, 0.0) if c == 7 else value

        for c in range(8):
            for k in range(PLANES):
                short = SHORT_AT + 5 * k
                f[k, c, 0:3, :] = jnp.zeros((3, 128), F32)
                f[k, c, 3:8, :] = piece(up, c, short, 5)
                f[k, c, 8:16, :] = piece(up, c, 8 * k, 8)
                f[k, c, 16:32, :] = q[k, c]
                f[k, c, 32:40, :] = piece(down, c, 8 * k, 8)
                f[k, c, 40:45, :] = piece(down, c, short, 5)
                f[k, c, 45:48, :] = jnp.zeros((3, 128), F32)
            for k in range(K):
                row = slice(k, k + 1)
                f[k, c, 15:16, :] += q[PLANES, c, row, :]
                f[k, c, 16:17, :] += piece(up, c, GUESS_AT + k, 1)
                f[k, c, 31:32, :] += piece(down, c, GUESS_AT + k, 1)
                f[k, c, 32:33, :] += q[PLANES + 1, c, row, :]

    parity_copy(even, on, off, assemble)
    clear_edges(xa, 48)
    clear_edges(xb, 48)
    scales(f, inv, ratio, 1.0)
    first_sweep(xa, f, inv, 48)
    second_sweep(xa, xb, f, inv, 48, 1.0)
    restrict(xb, f, inv, ratio, rs, gs, f1, 48, 1.0, 0, 24)
    for k in range(K):
        x0_out[k] = xb[k + 1, 1:7, 20:44, :]
    for k in range(PLANES):
        f0_out[k] = f[k, 1:7, 12:36, :]

    clear_edges(xc, 24)
    clear_edges(xd, 24)
    scales(f1, inv1, ratio1, 0.25)
    first_sweep(xc, f1, inv1, 24)
    second_sweep(xc, xd, f1, inv1, 24, 0.25)
    restrict(xd, f1, inv1, ratio1, rs1, gs1, f2_out, 24, 0.25, 4, 8)
    for k in range(K):
        x1_out[k] = xd[k + 1, :, 12:28, :]
    for k in range(PLANES):
        f1_out[k] = f1[k, :, 4:20, :]


def middle_kernel(own, on, off, x2_out, f2, chunk, xa, xb, inv, ratio, rs, gs, f3):
    even = lax.axis_index("gx") % 2 == 0

    def assemble(up, down):
        for k in range(PLANES):
            f2[k, :, 0:1, :] = jnp.zeros((2, 1, 128), F32)
            f2[k, :, 1:6, :] = up[k, :, 1:6, :]
            f2[k, :, 6:10, :] = own[k, :, 2:6, :]
            f2[k, :, 10:15, :] = down[k, :, 2:7, :]
            f2[k, :, 15:16, :] = jnp.zeros((2, 1, 128), F32)

    parity_copy(even, on, off, assemble)
    h = 0.25**2
    clear_edges(xa, 16)
    clear_edges(xb, 16)
    scales(f2, inv, ratio, h)
    first_sweep(xa, f2, inv, 16)
    second_sweep(xa, xb, f2, inv, 16, h)
    restrict(xb, f2, inv, ratio, rs, gs, f3, 16, h, 0, 8)
    for k in range(K):
        x2_out[k] = xb[k + 1, :, 8:24, :]
    rows = [f3[k, 0, 3:5, :] for k in range(PLANES)]
    rows.append(jnp.zeros((2, 128), F32))
    piece = jnp.concatenate(rows, axis=0)

    def fill(i, carry):
        chunk[i] = piece
        return carry

    lax.fori_loop(0, chunk.shape[0], fill, 0)


def add_copies(x, coarse, es, at_row, n, rows, first, count):
    chunks = coarse.shape[1]
    for k in range(K):
        for c in range(chunks):
            es[(k * chunks + c) * n : (k * chunks + c) * n + n, :] = coarse[k + 1, c, 8 + at_row : 8 + at_row + n, :]
    wide = exact_dot(es[...], copy_matrix(256))
    skip = (2 * n - rows) // 4
    used = rows // 2
    for k in range(K):
        for c in range(chunks):
            base = (k * chunks + c) * n + skip
            for half in range(2):
                fc = 2 * c + half - first
                if 0 <= fc < count:
                    e = wide[base : base + used, 128 * half : 128 * half + 128]
                    for p in range(2):
                        x[k + 1, fc, pl.ds(8 + p, used, stride=2), :] += e


def coarse_kernel(
    same, other, x2_in, f2, x1_in, f1, x0_in, f0, guess, updated, new_defect,
    f3, xa, xb, inv3, ratio3, rs3, gs3, f4, ya, yb, inv4, es3, es2, xc, xd, inv2, es1, xe, xf, inv1, es0, xg, xh, inv0,
):
    gx = lax.axis_index("gx")
    tiles = 2 * same.shape[0]
    for t in range(TILES):
        tile = gx - SIDE + t
        valid = jnp.logical_and(tile >= 0, tile < tiles)
        chip = jnp.clip(tile, 0, tiles - 1) // 2
        piece = jnp.where(valid, (same if t % 2 else other)[chip], 0.0)
        for k in range(PLANES):
            f3[k, 0, 2 * t : 2 * t + 2, :] = piece[2 * k : 2 * k + 2]
    for k in range(PLANES):
        f3[k, 0, 2 * TILES : 48, :] = jnp.zeros((48 - 2 * TILES, 128), F32)
    h = 0.25**3
    clear_edges(xa, 48)
    clear_edges(xb, 48)
    scales(f3, inv3, ratio3, h)
    first_sweep(xa, f3, inv3, 48)
    second_sweep(xa, xb, f3, inv3, 48, h)
    restrict(xb, f3, inv3, ratio3, rs3, gs3, f4, 48, h, 0, 24)

    h = 0.25**4
    clear_edges(ya, 24)
    clear_edges(yb, 24)
    scales(f4, inv4, None, h)
    first_sweep(ya, f4, inv4, 24)
    second_sweep(ya, yb, f4, inv4, 24, h)
    for _ in range(3):
        sweep(yb, ya, f4, inv4, 24, h)
        sweep(ya, yb, f4, inv4, 24, h)

    h = 0.25**3
    for k in range(K):
        es3[24 * k : 24 * k + 24, :] = yb[k + 1, 0, 8:32, :]
    wide = exact_dot(es3[...], copy_matrix(128))
    for k in range(K):
        for p in range(2):
            xb[k + 1, 0, pl.ds(8 + p, 24, stride=2), :] += wide[24 * k : 24 * k + 24]
    sweep(xb, xa, f3, inv3, 48, h)
    sweep(xa, xb, f3, inv3, 48, h)

    h = 0.25**2
    clear_edges(xc, 16)
    clear_edges(xd, 16)
    scales(f2, inv2, None, h)
    for k in range(K):
        xc[k + 1, :, 8:24, :] = x2_in[k]
    add_copies(xc, xb, es2, 19, 8, 16, 0, 2)
    sweep(xc, xd, f2, inv2, 16, h)
    sweep(xd, xc, f2, inv2, 16, h)

    h = 0.25
    clear_edges(xe, 16)
    clear_edges(xf, 16)
    scales(f1, inv1, None, h)
    for k in range(K):
        xe[k + 1, :, 8:24, :] = x1_in[k]
    add_copies(xe, xc, es1, 4, 8, 16, 0, 4)
    sweep(xe, xf, f1, inv1, 16, h)
    sweep(xf, xe, f1, inv1, 16, h)

    clear_edges(xg, 24)
    clear_edges(xh, 24)
    scales(f0, inv0, None, 1.0)
    for k in range(K):
        xg[k + 1, :, 8:32, :] = x0_in[k]
    add_copies(xg, xe, es0, 0, 16, 24, 1, 6)
    sweep(xg, xh, f0, inv0, 24, 1.0)
    sweep(xh, xg, f0, inv0, 24, 1.0)

    for k in range(K):
        for c, (v, hs, vs) in enumerate(stencil(xg, k, 16, 12)):
            if 1 <= c <= 4:
                vc = f0[VC, c, 4:20, :]
                center = 4.0 + 2.0 * vc + f0[BT, c, 4:20, :]
                cols = slice(128 * (c - 1), 128 * c)
                new_defect[k, :, cols] = f0[k, c, 4:20, :] - center * v + hs + vc * vs
                updated[k, :, cols] = guess[k, :, cols] + v


def call(kernel, name, outs, scratch, *operands, space=pltpu.VMEM, mib=48):
    spec = pl.BlockSpec(memory_space=pltpu.VMEM)
    return pl.pallas_call(
        kernel,
        name=name,
        out_shape=[jax.ShapeDtypeStruct(s, F32) for s in outs],
        in_specs=[pl.BlockSpec(memory_space=space)] * len(operands),
        out_specs=[spec] * len(outs),
        scratch_shapes=[pltpu.VMEM(s, F32) if isinstance(s, tuple) else s for s in scratch],
        compiler_params=pltpu.CompilerParams(vmem_limit_bytes=mib * 1024 * 1024),
    )(*operands)


def field(chunks, rows):
    return (K + 2, chunks, rows + 16, 128)


def shards(right_side, guess, vertical, breaking):
    nx, ny = lax.axis_size("gx"), lax.axis_size("gy")
    chip = [(i, i ^ 1) for i in range(nx)]
    gap = [(i, i + 1) for i in range(1, nx - 1, 2)]
    gap = gap + [(b, a) for a, b in gap]

    to_left, to_right = call(
        pack_kernel,
        "pack",
        [(Y_ROWS, 128), (Y_ROWS, 128)],
        [(K, 16, 512), (K, 16, 512), (16, 512), pltpu.VMEM((16, 512), jnp.int32), pltpu.SemaphoreType.DMA((4,))],
        right_side, guess, vertical, breaking,
        space=pltpu.HBM,
        mib=62,
    )
    from_right = lax.ppermute(to_left, "gy", [(j + 1, j) for j in range(ny - 1)])
    from_left = lax.ppermute(to_right, "gy", [(j, j + 1) for j in range(ny - 1)])
    q, to_on, to_off = call(
        widen_kernel,
        "widen",
        [(PLANES + 2, 8, 16, 128), (7, X_ROWS, 128), (7, X_ROWS, 128)],
        [],
        right_side, guess, vertical, breaking, from_left, from_right,
    )
    off = lax.ppermute(to_off, "gx", gap)
    on = lax.ppermute(to_on, "gx", chip)
    x0, f0, x1, f1, f2_own = call(
        fine_kernel,
        "fine",
        [(K, 6, 24, 128), (PLANES, 6, 24, 128), (K, 4, 16, 128), (PLANES, 4, 16, 128), (PLANES, 2, 8, 128)],
        [
            (PLANES, 8, 48, 128), field(8, 48), field(8, 48), (8, 48, 128), (8, 48, 128), (8, 64, 128), (K, 4 * 24, 256),
            (PLANES, 4, 24, 128), field(4, 24), field(4, 24), (4, 24, 128), (4, 24, 128), (4, 40, 128), (K, 2 * 8, 256),
        ],
        q, off, on,
    )
    off = lax.ppermute(f2_own, "gx", gap)
    on = lax.ppermute(f2_own, "gx", chip)
    x2, f2, chunk = call(
        middle_kernel,
        "middle",
        [(K, 2, 16, 128), (PLANES, 2, 16, 128), (nx // 2, 24, 128)],
        [field(2, 16), field(2, 16), (2, 16, 128), (2, 16, 128), (2, 32, 128), (K, 8, 256), (PLANES, 1, 8, 128)],
        f2_own, on, off,
    )
    same = lax.all_to_all(
        chunk, "gx", 0, 0, axis_index_groups=[list(range(0, nx, 2)), list(range(1, nx, 2))], tiled=True
    )
    other = lax.ppermute(same, "gx", chip)
    return tuple(
        call(
            coarse_kernel,
            "coarse",
            [(K, 16, 512), (K, 16, 512)],
            [
                (PLANES, 1, 48, 128), field(1, 48), field(1, 48), (1, 48, 128), (1, 48, 128), (1, 64, 128), (K, 24, 128),
                (PLANES, 1, 24, 128), field(1, 24), field(1, 24), (1, 24, 128), (K * 24, 128),
                (K * 8, 128), field(2, 16), field(2, 16), (2, 16, 128),
                (K * 2 * 8, 128), field(4, 16), field(4, 16), (4, 16, 128),
                (K * 4 * 16, 128), field(6, 24), field(6, 24), (6, 24, 128),
            ],
            same, other, x2, f2, x1, f1, x0, f0, guess,
        )
    )


def solution(mesh):
    in_specs = (P(None, "gx", "gy"), P(None, "gx", "gy"), P("gx", "gy"), P("gx", "gy"))
    out_specs = (P(None, "gx", "gy"), P(None, "gx", "gy"))
    return jax.shard_map(shards, mesh=mesh, in_specs=in_specs, out_specs=out_specs, check_vma=False)
```

```python
import jax
import jax.numpy as jnp
from jax import lax
from jax.experimental import pallas as pl
from jax.experimental.pallas import tpu as pltpu
from jax.sharding import PartitionSpec as P

K = 9
PLANES = K + 2
VC, BT = K, K + 1
TILES = 23
SIDE = TILES // 2
PLANE = 8
EXTRA = SIDE - PLANE
damping = 0.8
keep = 0.2
break_gain = 0.05
F32 = jnp.float32
BF16 = jnp.bfloat16

COLS_AT = 24 * PLANES
TOP_AT = COLS_AT + 16
BOTTOM_AT = TOP_AT + 16
FAR_AT = BOTTOM_AT + 16
Y_ROWS = FAR_AT + 16

SHORT_AT = 8 * PLANES
GUESS_AT = SHORT_AT + 5 * PLANES
X_ROWS = GUESS_AT + K


def lanes(rows):
    return lax.broadcasted_iota(jnp.int32, (rows, 128), 1)


def shifted(chunks):
    lane = lanes(chunks[0].shape[0])
    right = [pltpu.roll(v, 1, 1) for v in chunks]
    left = [pltpu.roll(v, 127, 1) for v in chunks]
    n = len(chunks)
    before = [jnp.where(lane == 0, right[c - 1], right[c]) if c else right[c] for c in range(n)]
    after = [jnp.where(lane == 127, left[c + 1], left[c]) if c < n - 1 else left[c] for c in range(n)]
    return before, after


def stencil(x, k, rows, at):
    count = x.shape[1]
    here = pl.ds(at, rows)
    v = [x[k + 1, c, here, :] for c in range(count)]
    before, after = shifted(v)
    out = []
    for c in range(count):
        hs = (x[k + 1, c, pl.ds(at - 1, rows), :] + x[k + 1, c, pl.ds(at + 1, rows), :]) + (before[c] + after[c])
        vs = x[k, c, here, :] + x[k + 2, c, here, :]
        out.append((v[c], hs, vs))
    return out


def clear_edges(x, rows):
    count, total = x.shape[1], x.shape[2]
    for k in (0, K + 1):
        x[k] = jnp.zeros((count, total, 128), F32)
    for k in range(1, K + 1):
        x[k, :, 0:8, :] = jnp.zeros((count, 8, 128), F32)
        x[k, :, 8 + rows : total, :] = jnp.zeros((count, total - 8 - rows, 128), F32)


def scales(f, inv, ratio, h):
    for c in range(f.shape[1]):
        vc = f[VC, c]
        center = 4.0 * h + 2.0 * vc + f[BT, c]
        inv[c] = jnp.where(vc > 0.0, damping / center, 0.0)
        if ratio is not None:
            ratio[c] = center * (1.0 / damping)


def first_sweep(x, f, inv, rows):
    for k in range(K):
        for c in range(f.shape[1]):
            x[k + 1, c, pl.ds(8, rows), :] = inv[c] * f[k, c]


def times(h, value):
    return value if h == 1.0 else h * value


def second_sweep(x, y, f, inv, rows, h):
    for k in range(K):
        for c, (v, hs, vs) in enumerate(stencil(x, k, rows, 8)):
            y[k + 1, c, pl.ds(8, rows), :] = (1.0 + keep) * v + inv[c] * (times(h, hs) + f[VC, c] * vs)


def sweep(x, y, f, inv, rows, h):
    for k in range(K):
        for c, (v, hs, vs) in enumerate(stencil(x, k, rows, 8)):
            y[k + 1, c, pl.ds(8, rows), :] = keep * v + inv[c] * (f[k, c] + times(h, hs) + f[VC, c] * vs)


def pair_matrix(inputs):
    i = lax.broadcasted_iota(jnp.int32, (inputs, 128), 0)
    j = lax.broadcasted_iota(jnp.int32, (inputs, 128), 1)
    return jnp.where((i == 2 * j) | (i == 2 * j + 1), 0.25, 0.0).astype(BF16)


def fold_matrix(inputs):
    i = lax.broadcasted_iota(jnp.int32, (inputs, 128), 0)
    d = i - 2 * lax.broadcasted_iota(jnp.int32, (inputs, 128), 1)
    inner = jnp.where((d == 0) | (d == 1), 0.375, 0.0)
    return jnp.where((d == -1) | (d == 2), 0.125, inner).astype(BF16)


def copy_matrix(outputs):
    i = lax.broadcasted_iota(jnp.int32, (128, outputs), 0)
    j = lax.broadcasted_iota(jnp.int32, (128, outputs), 1)
    return jnp.where((j == 2 * i) | (j == 2 * i + 1), 1.0, 0.0).astype(BF16)


def exact_dot(values, matrix, parts=3):
    total = None
    for _ in range(parts):
        part = values.astype(BF16)
        values = values - part.astype(F32)
        product = jnp.dot(part, matrix, preferred_element_type=F32)
        total = product if total is None else total + product
    return total


def restrict(x, f, inv, ratio, rs, gs, coarse, rows, h, base, n):
    count = f.shape[1]
    pairs = max(count // 2, 1)
    width = gs.shape[-1]
    lane = lanes(n)
    rs[:, 0:8, :] = jnp.zeros((count, 8, 128), F32)
    rs[:, 8 + rows : 16 + rows, :] = jnp.zeros((count, 8, 128), F32)

    def part(slot, c):
        return gs[slot, (c // 2) * n : (c // 2) * n + n, 128 * (c % 2) : 128 * (c % 2) + 128]

    def put(slot, c, value):
        gs[slot, (c // 2) * n : (c // 2) * n + n, 128 * (c % 2) : 128 * (c % 2) + 128] = value

    def residual(k, slot):
        for c, (v, hs, vs) in enumerate(stencil(x, k, rows, 8)):
            around = inv[c] * (f[k, c] + times(h, hs) + f[VC, c] * vs)
            rs[c, 8 : 8 + rows, :] = ratio[c] * (around - damping * v)
        for c in range(count):

            def pick(start):
                return rs[c, pl.ds(8 + base + start, n, stride=2), :]

            put(slot, c, (pick(-1) + 3.0 * (pick(0) + pick(1)) + pick(2)) * 0.125)

    def emit(k, slot, values):
        for j in range(pairs):
            value = values[j * n : j * n + n]
            if j > 0:
                value = value + jnp.where(lane == 0, 0.125 * pltpu.roll(part(slot, 2 * j - 1), 1, 1), 0.0)
            if j < pairs - 1:
                value = value + jnp.where(lane == 127, 0.125 * pltpu.roll(part(slot, 2 * j + 2), 127, 1), 0.0)
            coarse[k, j] = value

    matrix = fold_matrix(width)
    for k in range(K):
        residual(k, k)
    size = pairs * n
    values = exact_dot(gs[...].reshape(K * size, width), matrix, 2)
    for k in range(K):
        emit(k, k, values[k * size : k * size + size])
    for slot, k in enumerate((VC, BT)):
        for c in range(count):
            put(slot, c, f[k, c, pl.ds(base, n, stride=2), :] + f[k, c, pl.ds(base + 1, n, stride=2), :])
    values = exact_dot(gs[0:2].reshape(2 * pairs * n, width), pair_matrix(width))
    for slot, k in enumerate((VC, BT)):
        for j in range(pairs):
            at = (slot * pairs + j) * n
            coarse[k, j] = values[at : at + n]


def parity_copy(even, on, off, assemble):
    @pl.when(even)
    def _():
        assemble(off, on)

    @pl.when(jnp.logical_not(even))
    def _():
        assemble(on, off)


def own_defect(right_side, guess, vc, bt, k, left, right):
    v = guess[k]
    row = lax.broadcasted_iota(jnp.int32, v.shape, 0)
    col = lax.broadcasted_iota(jnp.int32, v.shape, 1)
    hs = jnp.where(row > 0, pltpu.roll(v, 1, 0), 0.0) + jnp.where(row < 15, pltpu.roll(v, 15, 0), 0.0)
    hs = hs + jnp.where(col > 0, pltpu.roll(v, 1, 1), left) + jnp.where(col < 511, pltpu.roll(v, 511, 1), right)
    vs = guess[1] if k == 0 else guess[K - 2] if k == K - 1 else guess[k - 1] + guess[k + 1]
    return right_side[k] - (4.0 + 2.0 * vc + bt) * v + hs + vc * vs


def pack_kernel(rs_in, g_in, vc_in, br_in, to_inside, to_across, right_side, guess, vertical, breaking, sems):
    pairs = ((vc_in, vertical), (br_in, breaking), (g_in, guess), (rs_in, right_side))
    copies = [pltpu.make_async_copy(a, b, sems.at[i]) for i, (a, b) in enumerate(pairs)]
    for copy in copies:
        copy.start()
    for copy in copies:
        copy.wait()
    lane = lanes(16)
    lane8 = lanes(8)
    vc = vertical[...]
    bt = break_gain * breaking[...].astype(F32)

    def pack_all(to_right, to_left):
        def pack(plane, field):
            near, far = field[:, 0:128], field[:, 128:256]
            to_left[24 * plane : 24 * plane + 16, :] = near
            to_left[24 * plane + 16 : 24 * plane + 24, :] = jnp.where(
                lane8 < 64, far[0:8], pltpu.roll(far[8:16], 64, 1)
            )
            near, far = field[:, 384:512], field[:, 256:384]
            to_right[24 * plane : 24 * plane + 16, :] = near
            to_right[24 * plane + 16 : 24 * plane + 24, :] = jnp.where(
                lane8 >= 64, far[0:8], pltpu.roll(far[8:16], 64, 1)
            )

        first = jnp.zeros((16, 128), F32)
        last = jnp.zeros((16, 128), F32)
        to_left[TOP_AT:Y_ROWS, :] = jnp.zeros((Y_ROWS - TOP_AT, 128), F32)
        to_right[TOP_AT:Y_ROWS, :] = jnp.zeros((Y_ROWS - TOP_AT, 128), F32)
        lane1 = lanes(1)
        for k in range(K):
            v = guess[k]
            f = own_defect(right_side, guess, vc, bt, k, 0.0, 0.0)
            pack(k, f)
            first = jnp.where(lane == k, jnp.broadcast_to(v[:, 0:1], (16, 128)), first)
            last = jnp.where(lane == k, jnp.broadcast_to(v[:, 511:512], (16, 128)), last)
            top, bottom = v[0:1], v[15:16]
            to_left[TOP_AT + k : TOP_AT + k + 1, :] = top[:, 0:128]
            to_left[BOTTOM_AT + k : BOTTOM_AT + k + 1, :] = bottom[:, 0:128]
            to_left[FAR_AT + k : FAR_AT + k + 1, :] = jnp.where(
                lane1 < 64, top[:, 128:256], pltpu.roll(bottom[:, 128:256], 64, 1)
            )
            to_right[TOP_AT + k : TOP_AT + k + 1, :] = top[:, 384:512]
            to_right[BOTTOM_AT + k : BOTTOM_AT + k + 1, :] = bottom[:, 384:512]
            to_right[FAR_AT + k : FAR_AT + k + 1, :] = jnp.where(
                lane1 >= 64, top[:, 256:384], pltpu.roll(bottom[:, 256:384], 64, 1)
            )
        pack(VC, vc)
        pack(BT, bt)
        to_left[COLS_AT : COLS_AT + 16, :] = first
        to_right[COLS_AT : COLS_AT + 16, :] = last

    parity_copy(lax.axis_index("gy") % 2 == 0, to_inside, to_across, lambda left, right: pack_all(right, left))


def widen_kernel(right_side, guess, vertical, breaking, across, inside, q, to_on, to_off):
    lane = lanes(16)

    def assemble(from_left, from_right):
        lane = lanes(16)
        lane8 = lanes(8)
        lane1 = lanes(1)
        left_cols = from_left[COLS_AT : COLS_AT + 16, :]
        right_cols = from_right[COLS_AT : COLS_AT + 16, :]
        vc = vertical[...]
        bt = break_gain * breaking[...].astype(F32)
        for k in range(PLANES):
            far = from_left[24 * k + 16 : 24 * k + 24, :]
            q[k, 0, 0:8, :] = jnp.where(lane8 >= 64, far, 0.0)
            q[k, 0, 8:16, :] = jnp.where(lane8 >= 64, pltpu.roll(far, 64, 1), 0.0)
            far = from_right[24 * k + 16 : 24 * k + 24, :]
            q[k, 7, 0:8, :] = jnp.where(lane8 < 64, far, 0.0)
            q[k, 7, 8:16, :] = jnp.where(lane8 < 64, pltpu.roll(far, 64, 1), 0.0)
            near_left = from_left[24 * k : 24 * k + 16, :]
            near_right = from_right[24 * k : 24 * k + 16, :]
            if k < K:
                v = guess[k]
                first = jnp.broadcast_to(v[:, 0:1], (16, 128))
                last = jnp.broadcast_to(v[:, 511:512], (16, 128))
                q[k, 1] = near_left + jnp.where(lane == 127, first, 0.0)
                q[k, 6] = near_right + jnp.where(lane == 0, last, 0.0)
                own = own_defect(right_side, guess, vc, bt, k, left_cols[:, k : k + 1], right_cols[:, k : k + 1])
            else:
                q[k, 1] = near_left
                q[k, 6] = near_right
                own = vc if k == VC else bt
            for c in range(4):
                q[k, 2 + c] = own[:, 128 * c : 128 * c + 128]
        for plane, row, near_at in ((PLANES, 0, TOP_AT), (PLANES + 1, 15, BOTTOM_AT)):
            for c in range(8):
                q[plane, c] = jnp.zeros((16, 128), F32)
            for k in range(K):
                at = slice(k, k + 1)
                v = guess[k, row : row + 1, :]
                for c in range(4):
                    q[plane, 2 + c, at, :] = v[:, 128 * c : 128 * c + 128]
                q[plane, 1, at, :] = from_left[near_at + k : near_at + k + 1, :]
                q[plane, 6, at, :] = from_right[near_at + k : near_at + k + 1, :]
                far_left = from_left[FAR_AT + k : FAR_AT + k + 1, :]
                far_right = from_right[FAR_AT + k : FAR_AT + k + 1, :]
                if plane == PLANES + 1:
                    far_left = pltpu.roll(far_left, 64, 1)
                    far_right = pltpu.roll(far_right, 64, 1)
                q[plane, 0, at, :] = jnp.where(lane1 >= 64, far_left, 0.0)
                q[plane, 7, at, :] = jnp.where(lane1 < 64, far_right, 0.0)

    parity_copy(lax.axis_index("gy") % 2 == 0, inside, across, assemble)

    def fill(buffer, long, short, plane):
        for c in range(7):
            for k in range(PLANES):
                piece = jnp.where(lane < 64, q[k, 7], q[k, 0]) if c == 0 else q[k, c]
                buffer[c, 8 * k : 8 * k + 8, :] = piece[long : long + 8]
                buffer[c, SHORT_AT + 5 * k : SHORT_AT + 5 * k + 5, :] = piece[short : short + 5]
            piece = jnp.where(lane < 64, q[plane, 7], q[plane, 0]) if c == 0 else q[plane, c]
            buffer[c, GUESS_AT : GUESS_AT + K, :] = piece[0:K]

    def fill_both(to_up, to_down):
        fill(to_up, 0, 8, PLANES)
        fill(to_down, 8, 3, PLANES + 1)

    parity_copy(lax.axis_index("gx") % 2 == 0, to_on, to_off, fill_both)


def fine_kernel(q, off, on, x0_out, f0_out, x1_out, f1_out, f2_out, f, xa, xb, inv, ratio, rs, gs, f1, xc, xd, inv1, ratio1, rs1, gs1):
    even = lax.axis_index("gx") % 2 == 0

    def assemble(up, down):
        lane = lanes(8)

        def piece(buffer, c, at, n):
            value = buffer[min(c % 7, c), at : at + n, :]
            if c == 0:
                return jnp.where(lane[0:n] >= 64, value, 0.0)
            return jnp.where(lane[0:n] < 64, value, 0.0) if c == 7 else value

        for c in range(8):
            for k in range(PLANES):
                short = SHORT_AT + 5 * k
                f[k, c, 0:3, :] = jnp.zeros((3, 128), F32)
                f[k, c, 3:8, :] = piece(up, c, short, 5)
                f[k, c, 8:16, :] = piece(up, c, 8 * k, 8)
                f[k, c, 16:32, :] = q[k, c]
                f[k, c, 32:40, :] = piece(down, c, 8 * k, 8)
                f[k, c, 40:45, :] = piece(down, c, short, 5)
                f[k, c, 45:48, :] = jnp.zeros((3, 128), F32)
            for k in range(K):
                row = slice(k, k + 1)
                f[k, c, 15:16, :] += q[PLANES, c, row, :]
                f[k, c, 16:17, :] += piece(up, c, GUESS_AT + k, 1)
                f[k, c, 31:32, :] += piece(down, c, GUESS_AT + k, 1)
                f[k, c, 32:33, :] += q[PLANES + 1, c, row, :]

    parity_copy(even, on, off, assemble)
    clear_edges(xa, 48)
    clear_edges(xb, 48)
    scales(f, inv, ratio, 1.0)
    first_sweep(xa, f, inv, 48)
    second_sweep(xa, xb, f, inv, 48, 1.0)
    restrict(xb, f, inv, ratio, rs, gs, f1, 48, 1.0, 0, 24)
    for k in range(K):
        x0_out[k] = xb[k + 1, 1:7, 20:44, :]
    for k in range(PLANES):
        f0_out[k] = f[k, 1:7, 12:36, :]

    clear_edges(xc, 24)
    clear_edges(xd, 24)
    scales(f1, inv1, ratio1, 0.25)
    first_sweep(xc, f1, inv1, 24)
    second_sweep(xc, xd, f1, inv1, 24, 0.25)
    restrict(xd, f1, inv1, ratio1, rs1, gs1, f2_out, 24, 0.25, 4, 8)
    for k in range(K):
        x1_out[k] = xd[k + 1, :, 12:28, :]
    for k in range(PLANES):
        f1_out[k] = f1[k, :, 4:20, :]


def middle_kernel(own, on, off, x2_out, f2, chunk, xa, xb, inv, ratio, rs, gs, f3):
    even = lax.axis_index("gx") % 2 == 0

    def assemble(up, down):
        for k in range(PLANES):
            f2[k, :, 0:1, :] = jnp.zeros((2, 1, 128), F32)
            f2[k, :, 1:6, :] = up[k, :, 1:6, :]
            f2[k, :, 6:10, :] = own[k, :, 2:6, :]
            f2[k, :, 10:15, :] = down[k, :, 2:7, :]
            f2[k, :, 15:16, :] = jnp.zeros((2, 1, 128), F32)

    parity_copy(even, on, off, assemble)
    h = 0.25**2
    clear_edges(xa, 16)
    clear_edges(xb, 16)
    scales(f2, inv, ratio, h)
    first_sweep(xa, f2, inv, 16)
    second_sweep(xa, xb, f2, inv, 16, h)
    restrict(xb, f2, inv, ratio, rs, gs, f3, 16, h, 0, 8)
    for k in range(K):
        x2_out[k] = xb[k + 1, :, 8:24, :]
    rows = [f3[k, 0, 3:5, :] for k in range(PLANES)]
    rows.append(jnp.zeros((2, 128), F32))
    piece = jnp.concatenate(rows, axis=0)

    def fill(i, carry):
        chunk[i] = piece
        return carry

    lax.fori_loop(0, chunk.shape[0], fill, 0)


def add_copies(x, coarse, es, at_row, n, rows, first, count):
    chunks = coarse.shape[1]
    for k in range(K):
        for c in range(chunks):
            es[(k * chunks + c) * n : (k * chunks + c) * n + n, :] = coarse[k + 1, c, 8 + at_row : 8 + at_row + n, :]
    wide = exact_dot(es[...], copy_matrix(256))
    skip = (2 * n - rows) // 4
    used = rows // 2
    for k in range(K):
        for c in range(chunks):
            base = (k * chunks + c) * n + skip
            for half in range(2):
                fc = 2 * c + half - first
                if 0 <= fc < count:
                    e = wide[base : base + used, 128 * half : 128 * half + 128]
                    for p in range(2):
                        x[k + 1, fc, pl.ds(8 + p, used, stride=2), :] += e


def edge_kernel(plane, copy, edge):
    copy[...] = plane[...]
    first = lax.axis_index("gx") % PLANE < PLANE // 2

    @pl.when(first)
    def _():
        edge[...] = plane[PLANE - EXTRA : PLANE]

    @pl.when(jnp.logical_not(first))
    def _():
        edge[...] = plane[0:EXTRA]


def coarse_kernel(
    plane, beyond, before, after, x2_in, f2, x1_in, f1, x0_in, f0, guess, updated, new_defect,
    window, f3, xa, xb, inv3, ratio3, rs3, gs3, f4, ya, yb, inv4, es3, es2, xc, xd, inv2, es1, xe, xf, inv1, es0, xg, xh, inv0,
):
    gx = lax.axis_index("gx")
    tiles = lax.axis_size("gx")
    place = gx % PLANE
    above, below = EXTRA, EXTRA + 2 * PLANE

    window[above : above + PLANE] = before[...]
    window[above + PLANE : below] = plane[...]
    window[below : below + PLANE] = after[...]

    @pl.when(place < PLANE // 2)
    def _():
        window[0:EXTRA] = beyond[...]

    @pl.when(place >= PLANE // 2)
    def _():
        window[below + PLANE : below + PLANE + EXTRA] = beyond[...]

    for t in range(TILES):
        tile = gx - SIDE + t
        valid = jnp.logical_and(tile >= 0, tile < tiles)
        piece = jnp.where(valid, window[place + t], 0.0)
        for k in range(PLANES):
            f3[k, 0, 2 * t : 2 * t + 2, :] = piece[2 * k : 2 * k + 2]
    for k in range(PLANES):
        f3[k, 0, 2 * TILES : 48, :] = jnp.zeros((48 - 2 * TILES, 128), F32)
    h = 0.25**3
    clear_edges(xa, 48)
    clear_edges(xb, 48)
    scales(f3, inv3, ratio3, h)
    first_sweep(xa, f3, inv3, 48)
    second_sweep(xa, xb, f3, inv3, 48, h)
    restrict(xb, f3, inv3, ratio3, rs3, gs3, f4, 48, h, 0, 24)

    h = 0.25**4
    clear_edges(ya, 24)
    clear_edges(yb, 24)
    scales(f4, inv4, None, h)
    first_sweep(ya, f4, inv4, 24)
    second_sweep(ya, yb, f4, inv4, 24, h)
    for _ in range(3):
        sweep(yb, ya, f4, inv4, 24, h)
        sweep(ya, yb, f4, inv4, 24, h)

    h = 0.25**3
    for k in range(K):
        es3[24 * k : 24 * k + 24, :] = yb[k + 1, 0, 8:32, :]
    wide = exact_dot(es3[...], copy_matrix(128))
    for k in range(K):
        for p in range(2):
            xb[k + 1, 0, pl.ds(8 + p, 24, stride=2), :] += wide[24 * k : 24 * k + 24]
    sweep(xb, xa, f3, inv3, 48, h)
    sweep(xa, xb, f3, inv3, 48, h)

    h = 0.25**2
    clear_edges(xc, 16)
    clear_edges(xd, 16)
    scales(f2, inv2, None, h)
    for k in range(K):
        xc[k + 1, :, 8:24, :] = x2_in[k]
    add_copies(xc, xb, es2, 19, 8, 16, 0, 2)
    sweep(xc, xd, f2, inv2, 16, h)
    sweep(xd, xc, f2, inv2, 16, h)

    h = 0.25
    clear_edges(xe, 16)
    clear_edges(xf, 16)
    scales(f1, inv1, None, h)
    for k in range(K):
        xe[k + 1, :, 8:24, :] = x1_in[k]
    add_copies(xe, xc, es1, 4, 8, 16, 0, 4)
    sweep(xe, xf, f1, inv1, 16, h)
    sweep(xf, xe, f1, inv1, 16, h)

    clear_edges(xg, 24)
    clear_edges(xh, 24)
    scales(f0, inv0, None, 1.0)
    for k in range(K):
        xg[k + 1, :, 8:32, :] = x0_in[k]
    add_copies(xg, xe, es0, 0, 16, 24, 1, 6)
    sweep(xg, xh, f0, inv0, 24, 1.0)
    sweep(xh, xg, f0, inv0, 24, 1.0)

    for k in range(K):
        for c, (v, hs, vs) in enumerate(stencil(xg, k, 16, 12)):
            if 1 <= c <= 4:
                vc = f0[VC, c, 4:20, :]
                center = 4.0 + 2.0 * vc + f0[BT, c, 4:20, :]
                cols = slice(128 * (c - 1), 128 * c)
                new_defect[k, :, cols] = f0[k, c, 4:20, :] - center * v + hs + vc * vs
                updated[k, :, cols] = guess[k, :, cols] + v


def call(kernel, name, outs, scratch, *operands, space=pltpu.VMEM, mib=48):
    spec = pl.BlockSpec(memory_space=pltpu.VMEM)
    return pl.pallas_call(
        kernel,
        name=name,
        out_shape=[jax.ShapeDtypeStruct(s, F32) for s in outs],
        in_specs=[pl.BlockSpec(memory_space=space)] * len(operands),
        out_specs=[spec] * len(outs),
        scratch_shapes=[pltpu.VMEM(s, F32) if isinstance(s, tuple) else s for s in scratch],
        compiler_params=pltpu.CompilerParams(vmem_limit_bytes=mib * 1024 * 1024),
    )(*operands)


def field(chunks, rows):
    return (K + 2, chunks, rows + 16, 128)


def shards(right_side, guess, vertical, breaking):
    nx, ny = lax.axis_size("gx"), lax.axis_size("gy")
    chip = [(i, i ^ 1) for i in range(nx)]
    gap = [(i, i + 1) for i in range(1, nx - 1, 2)]
    gap = gap + [(b, a) for a, b in gap]

    to_inside, to_across = call(
        pack_kernel,
        "pack",
        [(Y_ROWS, 128), (Y_ROWS, 128)],
        [(K, 16, 512), (K, 16, 512), (16, 512), pltpu.VMEM((16, 512), jnp.int32), pltpu.SemaphoreType.DMA((4,))],
        right_side, guess, vertical, breaking,
        space=pltpu.HBM,
        mib=62,
    )
    inside = [(j, j ^ 1) for j in range(ny)]
    across = [(j, j + 1) for j in range(1, ny - 1, 2)]
    across = lax.ppermute(to_across, "gy", across + [(b, a) for a, b in across])
    inside = lax.ppermute(to_inside, "gy", inside)
    q, to_on, to_off = call(
        widen_kernel,
        "widen",
        [(PLANES + 2, 8, 16, 128), (7, X_ROWS, 128), (7, X_ROWS, 128)],
        [],
        right_side, guess, vertical, breaking, across, inside,
    )
    off = lax.ppermute(to_off, "gx", gap)
    on = lax.ppermute(to_on, "gx", chip)
    x0, f0, x1, f1, f2_own = call(
        fine_kernel,
        "fine",
        [(K, 6, 24, 128), (PLANES, 6, 24, 128), (K, 4, 16, 128), (PLANES, 4, 16, 128), (PLANES, 2, 8, 128)],
        [
            (PLANES, 8, 48, 128), field(8, 48), field(8, 48), (8, 48, 128), (8, 48, 128), (8, 64, 128), (K, 4 * 24, 256),
            (PLANES, 4, 24, 128), field(4, 24), field(4, 24), (4, 24, 128), (4, 24, 128), (4, 40, 128), (K, 2 * 8, 256),
        ],
        q, off, on,
    )
    off = lax.ppermute(f2_own, "gx", gap)
    on = lax.ppermute(f2_own, "gx", chip)
    x2, f2, chunk = call(
        middle_kernel,
        "middle",
        [(K, 2, 16, 128), (PLANES, 2, 16, 128), (PLANE, 24, 128)],
        [field(2, 16), field(2, 16), (2, 16, 128), (2, 16, 128), (2, 32, 128), (K, 8, 256), (PLANES, 1, 8, 128)],
        f2_own, on, off,
    )
    groups = [list(range(i, i + PLANE)) for i in range(0, nx, PLANE)]
    plane = lax.all_to_all(chunk, "gx", 0, 0, axis_index_groups=groups, tiled=True)
    plane, edge = call(edge_kernel, "edge", [(PLANE, 24, 128), (EXTRA, 24, 128)], [], plane)
    far = [(i, i + 2 * PLANE) for i in range(nx - 2 * PLANE) if i % PLANE < EXTRA]
    far += [(i, i - 2 * PLANE) for i in range(2 * PLANE, nx) if i % PLANE >= PLANE - EXTRA]
    beyond = lax.ppermute(edge, "gx", far)
    before = lax.ppermute(plane, "gx", [(i, i + PLANE) for i in range(nx - PLANE)])
    after = lax.ppermute(plane, "gx", [(i + PLANE, i) for i in range(nx - PLANE)])
    return tuple(
        call(
            coarse_kernel,
            "coarse",
            [(K, 16, 512), (K, 16, 512)],
            [
                (2 * EXTRA + 3 * PLANE, 24, 128),
                (PLANES, 1, 48, 128), field(1, 48), field(1, 48), (1, 48, 128), (1, 48, 128), (1, 64, 128), (K, 24, 128),
                (PLANES, 1, 24, 128), field(1, 24), field(1, 24), (1, 24, 128), (K * 24, 128),
                (K * 8, 128), field(2, 16), field(2, 16), (2, 16, 128),
                (K * 2 * 8, 128), field(4, 16), field(4, 16), (4, 16, 128),
                (K * 4 * 16, 128), field(6, 24), field(6, 24), (6, 24, 128),
            ],
            plane, beyond, before, after, x2, f2, x1, f1, x0, f0, guess,
        )
    )


def solution(mesh):
    in_specs = (P(None, "gx", "gy"), P(None, "gx", "gy"), P("gx", "gy"), P("gx", "gy"))
    out_specs = (P(None, "gx", "gy"), P(None, "gx", "gy"))
    return jax.shard_map(shards, mesh=mesh, in_specs=in_specs, out_specs=out_specs, check_vma=False)
```

```python
import jax
import jax.numpy as jnp
from jax import lax
from jax.experimental import pallas as pl
from jax.experimental.pallas import tpu as pltpu
from jax.sharding import PartitionSpec as P

K = 9
PLANES = K + 2
VC, BT = K, K + 1
TILES = 23
SIDE = TILES // 2
PLANE = 8
EXTRA = SIDE - PLANE
damping = 0.8
keep = 0.2
break_gain = 0.05
F32 = jnp.float32
BF16 = jnp.bfloat16

COLS_AT = 24 * PLANES
TOP_AT = COLS_AT + 16
BOTTOM_AT = TOP_AT + 16
FAR_AT = BOTTOM_AT + 16
Y_ROWS = FAR_AT + 16

SHORT_AT = 8 * PLANES
GUESS_AT = SHORT_AT + 5 * PLANES
X_ROWS = GUESS_AT + K


def lanes(rows):
    return lax.broadcasted_iota(jnp.int32, (rows, 128), 1)


def shifted(chunks):
    lane = lanes(chunks[0].shape[0])
    right = [pltpu.roll(v, 1, 1) for v in chunks]
    left = [pltpu.roll(v, 127, 1) for v in chunks]
    n = len(chunks)
    before = [jnp.where(lane == 0, right[c - 1], right[c]) if c else right[c] for c in range(n)]
    after = [jnp.where(lane == 127, left[c + 1], left[c]) if c < n - 1 else left[c] for c in range(n)]
    return before, after


def stencil(x, k, rows, at):
    count = x.shape[1]
    here = pl.ds(at, rows)
    v = [x[k + 1, c, here, :] for c in range(count)]
    before, after = shifted(v)
    out = []
    for c in range(count):
        hs = (x[k + 1, c, pl.ds(at - 1, rows), :] + x[k + 1, c, pl.ds(at + 1, rows), :]) + (before[c] + after[c])
        vs = x[k, c, here, :] + x[k + 2, c, here, :]
        out.append((v[c], hs, vs))
    return out


def clear_edges(x, rows):
    count, total = x.shape[1], x.shape[2]
    for k in (0, K + 1):
        x[k] = jnp.zeros((count, total, 128), F32)
    for k in range(1, K + 1):
        x[k, :, 0:8, :] = jnp.zeros((count, 8, 128), F32)
        x[k, :, 8 + rows : total, :] = jnp.zeros((count, total - 8 - rows, 128), F32)


def scales(f, inv, ratio, h):
    for c in range(f.shape[1]):
        vc = f[VC, c]
        center = 4.0 * h + 2.0 * vc + f[BT, c]
        inv[c] = jnp.where(vc > 0.0, damping / center, 0.0)
        if ratio is not None:
            ratio[c] = center * (1.0 / damping)


def first_sweep(x, f, inv, rows):
    for k in range(K):
        for c in range(f.shape[1]):
            x[k + 1, c, pl.ds(8, rows), :] = inv[c] * f[k, c]


def times(h, value):
    return value if h == 1.0 else h * value


def second_sweep(x, y, f, inv, rows, h):
    for k in range(K):
        for c, (v, hs, vs) in enumerate(stencil(x, k, rows, 8)):
            y[k + 1, c, pl.ds(8, rows), :] = (1.0 + keep) * v + inv[c] * (times(h, hs) + f[VC, c] * vs)


def sweep(x, y, f, inv, rows, h):
    for k in range(K):
        for c, (v, hs, vs) in enumerate(stencil(x, k, rows, 8)):
            y[k + 1, c, pl.ds(8, rows), :] = keep * v + inv[c] * (f[k, c] + times(h, hs) + f[VC, c] * vs)


def pair_matrix(inputs):
    i = lax.broadcasted_iota(jnp.int32, (inputs, 128), 0)
    j = lax.broadcasted_iota(jnp.int32, (inputs, 128), 1)
    return jnp.where((i == 2 * j) | (i == 2 * j + 1), 0.25, 0.0).astype(BF16)


def fold_matrix(inputs):
    i = lax.broadcasted_iota(jnp.int32, (inputs, 128), 0)
    d = i - 2 * lax.broadcasted_iota(jnp.int32, (inputs, 128), 1)
    inner = jnp.where((d == 0) | (d == 1), 0.375, 0.0)
    return jnp.where((d == -1) | (d == 2), 0.125, inner).astype(BF16)


def copy_matrix(outputs):
    i = lax.broadcasted_iota(jnp.int32, (128, outputs), 0)
    j = lax.broadcasted_iota(jnp.int32, (128, outputs), 1)
    return jnp.where((j == 2 * i) | (j == 2 * i + 1), 1.0, 0.0).astype(BF16)


def exact_dot(values, matrix, parts=3):
    total = None
    for _ in range(parts):
        part = values.astype(BF16)
        values = values - part.astype(F32)
        product = jnp.dot(part, matrix, preferred_element_type=F32)
        total = product if total is None else total + product
    return total


def restrict(x, f, inv, ratio, rs, gs, coarse, rows, h, base, n):
    count = f.shape[1]
    pairs = max(count // 2, 1)
    width = gs.shape[-1]
    lane = lanes(n)
    rs[:, 0:8, :] = jnp.zeros((count, 8, 128), F32)
    rs[:, 8 + rows : 16 + rows, :] = jnp.zeros((count, 8, 128), F32)

    def part(slot, c):
        return gs[slot, (c // 2) * n : (c // 2) * n + n, 128 * (c % 2) : 128 * (c % 2) + 128]

    def put(slot, c, value):
        gs[slot, (c // 2) * n : (c // 2) * n + n, 128 * (c % 2) : 128 * (c % 2) + 128] = value

    def residual(k, slot):
        for c, (v, hs, vs) in enumerate(stencil(x, k, rows, 8)):
            around = inv[c] * (f[k, c] + times(h, hs) + f[VC, c] * vs)
            rs[c, 8 : 8 + rows, :] = ratio[c] * (around - damping * v)
        for c in range(count):

            def pick(start):
                return rs[c, pl.ds(8 + base + start, n, stride=2), :]

            put(slot, c, (pick(-1) + 3.0 * (pick(0) + pick(1)) + pick(2)) * 0.125)

    def emit(k, slot, values):
        for j in range(pairs):
            value = values[j * n : j * n + n]
            if j > 0:
                value = value + jnp.where(lane == 0, 0.125 * pltpu.roll(part(slot, 2 * j - 1), 1, 1), 0.0)
            if j < pairs - 1:
                value = value + jnp.where(lane == 127, 0.125 * pltpu.roll(part(slot, 2 * j + 2), 127, 1), 0.0)
            coarse[k, j] = value

    matrix = fold_matrix(width)
    for k in range(K):
        residual(k, k)
    size = pairs * n
    values = exact_dot(gs[...].reshape(K * size, width), matrix, 2)
    for k in range(K):
        emit(k, k, values[k * size : k * size + size])
    for slot, k in enumerate((VC, BT)):
        for c in range(count):
            put(slot, c, f[k, c, pl.ds(base, n, stride=2), :] + f[k, c, pl.ds(base + 1, n, stride=2), :])
    values = exact_dot(gs[0:2].reshape(2 * pairs * n, width), pair_matrix(width))
    for slot, k in enumerate((VC, BT)):
        for j in range(pairs):
            at = (slot * pairs + j) * n
            coarse[k, j] = values[at : at + n]


def parity_copy(even, on, off, assemble):
    @pl.when(even)
    def _():
        assemble(off, on)

    @pl.when(jnp.logical_not(even))
    def _():
        assemble(on, off)


def own_defect(right_side, guess, vc, bt, k, left, right):
    v = guess[k]
    row = lax.broadcasted_iota(jnp.int32, v.shape, 0)
    col = lax.broadcasted_iota(jnp.int32, v.shape, 1)
    hs = jnp.where(row > 0, pltpu.roll(v, 1, 0), 0.0) + jnp.where(row < 15, pltpu.roll(v, 15, 0), 0.0)
    hs = hs + jnp.where(col > 0, pltpu.roll(v, 1, 1), left) + jnp.where(col < 511, pltpu.roll(v, 511, 1), right)
    vs = guess[1] if k == 0 else guess[K - 2] if k == K - 1 else guess[k - 1] + guess[k + 1]
    return right_side[k] - (4.0 + 2.0 * vc + bt) * v + hs + vc * vs


def pack_kernel(rs_in, g_in, vc_in, br_in, to_inside, to_across, right_side, guess, vertical, breaking, sems):
    pairs = ((vc_in, vertical), (br_in, breaking), (g_in, guess), (rs_in, right_side))
    copies = [pltpu.make_async_copy(a, b, sems.at[i]) for i, (a, b) in enumerate(pairs)]
    for copy in copies:
        copy.start()
    for copy in copies:
        copy.wait()
    lane = lanes(16)
    lane8 = lanes(8)
    vc = vertical[...]
    bt = break_gain * breaking[...].astype(F32)

    def pack_all(to_right, to_left):
        def pack(plane, field):
            near, far = field[:, 0:128], field[:, 128:256]
            to_left[24 * plane : 24 * plane + 16, :] = near
            to_left[24 * plane + 16 : 24 * plane + 24, :] = jnp.where(
                lane8 < 64, far[0:8], pltpu.roll(far[8:16], 64, 1)
            )
            near, far = field[:, 384:512], field[:, 256:384]
            to_right[24 * plane : 24 * plane + 16, :] = near
            to_right[24 * plane + 16 : 24 * plane + 24, :] = jnp.where(
                lane8 >= 64, far[0:8], pltpu.roll(far[8:16], 64, 1)
            )

        first = jnp.zeros((16, 128), F32)
        last = jnp.zeros((16, 128), F32)
        to_left[TOP_AT:Y_ROWS, :] = jnp.zeros((Y_ROWS - TOP_AT, 128), F32)
        to_right[TOP_AT:Y_ROWS, :] = jnp.zeros((Y_ROWS - TOP_AT, 128), F32)
        lane1 = lanes(1)
        for k in range(K):
            v = guess[k]
            f = own_defect(right_side, guess, vc, bt, k, 0.0, 0.0)
            pack(k, f)
            first = jnp.where(lane == k, jnp.broadcast_to(v[:, 0:1], (16, 128)), first)
            last = jnp.where(lane == k, jnp.broadcast_to(v[:, 511:512], (16, 128)), last)
            top, bottom = v[0:1], v[15:16]
            to_left[TOP_AT + k : TOP_AT + k + 1, :] = top[:, 0:128]
            to_left[BOTTOM_AT + k : BOTTOM_AT + k + 1, :] = bottom[:, 0:128]
            to_left[FAR_AT + k : FAR_AT + k + 1, :] = jnp.where(
                lane1 < 64, top[:, 128:256], pltpu.roll(bottom[:, 128:256], 64, 1)
            )
            to_right[TOP_AT + k : TOP_AT + k + 1, :] = top[:, 384:512]
            to_right[BOTTOM_AT + k : BOTTOM_AT + k + 1, :] = bottom[:, 384:512]
            to_right[FAR_AT + k : FAR_AT + k + 1, :] = jnp.where(
                lane1 >= 64, top[:, 256:384], pltpu.roll(bottom[:, 256:384], 64, 1)
            )
        pack(VC, vc)
        pack(BT, bt)
        to_left[COLS_AT : COLS_AT + 16, :] = first
        to_right[COLS_AT : COLS_AT + 16, :] = last

    parity_copy(lax.axis_index("gy") % 2 == 0, to_inside, to_across, lambda left, right: pack_all(right, left))


def widen_kernel(right_side, guess, vertical, breaking, inside, across, q, to_on, to_off):
    lane = lanes(16)

    def assemble(from_left, from_right):
        lane = lanes(16)
        lane8 = lanes(8)
        lane1 = lanes(1)
        left_cols = from_left[COLS_AT : COLS_AT + 16, :]
        right_cols = from_right[COLS_AT : COLS_AT + 16, :]
        vc = vertical[...]
        bt = break_gain * breaking[...].astype(F32)
        for k in range(PLANES):
            far = from_left[24 * k + 16 : 24 * k + 24, :]
            q[k, 0, 0:8, :] = jnp.where(lane8 >= 64, far, 0.0)
            q[k, 0, 8:16, :] = jnp.where(lane8 >= 64, pltpu.roll(far, 64, 1), 0.0)
            far = from_right[24 * k + 16 : 24 * k + 24, :]
            q[k, 7, 0:8, :] = jnp.where(lane8 < 64, far, 0.0)
            q[k, 7, 8:16, :] = jnp.where(lane8 < 64, pltpu.roll(far, 64, 1), 0.0)
            near_left = from_left[24 * k : 24 * k + 16, :]
            near_right = from_right[24 * k : 24 * k + 16, :]
            if k < K:
                v = guess[k]
                first = jnp.broadcast_to(v[:, 0:1], (16, 128))
                last = jnp.broadcast_to(v[:, 511:512], (16, 128))
                q[k, 1] = near_left + jnp.where(lane == 127, first, 0.0)
                q[k, 6] = near_right + jnp.where(lane == 0, last, 0.0)
                own = own_defect(right_side, guess, vc, bt, k, left_cols[:, k : k + 1], right_cols[:, k : k + 1])
            else:
                q[k, 1] = near_left
                q[k, 6] = near_right
                own = vc if k == VC else bt
            for c in range(4):
                q[k, 2 + c] = own[:, 128 * c : 128 * c + 128]
        for plane, row, near_at in ((PLANES, 0, TOP_AT), (PLANES + 1, 15, BOTTOM_AT)):
            for c in range(8):
                q[plane, c] = jnp.zeros((16, 128), F32)
            for k in range(K):
                at = slice(k, k + 1)
                v = guess[k, row : row + 1, :]
                for c in range(4):
                    q[plane, 2 + c, at, :] = v[:, 128 * c : 128 * c + 128]
                q[plane, 1, at, :] = from_left[near_at + k : near_at + k + 1, :]
                q[plane, 6, at, :] = from_right[near_at + k : near_at + k + 1, :]
                far_left = from_left[FAR_AT + k : FAR_AT + k + 1, :]
                far_right = from_right[FAR_AT + k : FAR_AT + k + 1, :]
                if plane == PLANES + 1:
                    far_left = pltpu.roll(far_left, 64, 1)
                    far_right = pltpu.roll(far_right, 64, 1)
                q[plane, 0, at, :] = jnp.where(lane1 >= 64, far_left, 0.0)
                q[plane, 7, at, :] = jnp.where(lane1 < 64, far_right, 0.0)

    parity_copy(lax.axis_index("gy") % 2 == 0, inside, across, assemble)

    def fill(buffer, long, short, plane):
        for c in range(7):
            for k in range(PLANES):
                piece = jnp.where(lane < 64, q[k, 7], q[k, 0]) if c == 0 else q[k, c]
                buffer[c, 8 * k : 8 * k + 8, :] = piece[long : long + 8]
                buffer[c, SHORT_AT + 5 * k : SHORT_AT + 5 * k + 5, :] = piece[short : short + 5]
            piece = jnp.where(lane < 64, q[plane, 7], q[plane, 0]) if c == 0 else q[plane, c]
            buffer[c, GUESS_AT : GUESS_AT + K, :] = piece[0:K]

    def fill_both(to_up, to_down):
        fill(to_up, 0, 8, PLANES)
        fill(to_down, 8, 3, PLANES + 1)

    parity_copy(lax.axis_index("gx") % 2 == 0, to_on, to_off, fill_both)


def fine_kernel(q, off, on, x0_out, f0_out, x1_out, f1_out, f2_out, f, xa, xb, inv, ratio, rs, gs, f1, xc, xd, inv1, ratio1, rs1, gs1):
    even = lax.axis_index("gx") % 2 == 0

    def assemble(up, down):
        lane = lanes(8)

        def piece(buffer, c, at, n):
            value = buffer[min(c % 7, c), at : at + n, :]
            if c == 0:
                return jnp.where(lane[0:n] >= 64, value, 0.0)
            return jnp.where(lane[0:n] < 64, value, 0.0) if c == 7 else value

        for c in range(8):
            for k in range(PLANES):
                short = SHORT_AT + 5 * k
                f[k, c, 0:3, :] = jnp.zeros((3, 128), F32)
                f[k, c, 3:8, :] = piece(up, c, short, 5)
                f[k, c, 8:16, :] = piece(up, c, 8 * k, 8)
                f[k, c, 16:32, :] = q[k, c]
                f[k, c, 32:40, :] = piece(down, c, 8 * k, 8)
                f[k, c, 40:45, :] = piece(down, c, short, 5)
                f[k, c, 45:48, :] = jnp.zeros((3, 128), F32)
            for k in range(K):
                row = slice(k, k + 1)
                f[k, c, 15:16, :] += q[PLANES, c, row, :]
                f[k, c, 16:17, :] += piece(up, c, GUESS_AT + k, 1)
                f[k, c, 31:32, :] += piece(down, c, GUESS_AT + k, 1)
                f[k, c, 32:33, :] += q[PLANES + 1, c, row, :]

    parity_copy(even, on, off, assemble)
    clear_edges(xa, 48)
    clear_edges(xb, 48)
    scales(f, inv, ratio, 1.0)
    first_sweep(xa, f, inv, 48)
    second_sweep(xa, xb, f, inv, 48, 1.0)
    restrict(xb, f, inv, ratio, rs, gs, f1, 48, 1.0, 0, 24)
    for k in range(K):
        x0_out[k] = xb[k + 1, 1:7, 20:44, :]
    for k in range(PLANES):
        f0_out[k] = f[k, 1:7, 12:36, :]

    clear_edges(xc, 24)
    clear_edges(xd, 24)
    scales(f1, inv1, ratio1, 0.25)
    first_sweep(xc, f1, inv1, 24)
    second_sweep(xc, xd, f1, inv1, 24, 0.25)
    restrict(xd, f1, inv1, ratio1, rs1, gs1, f2_out, 24, 0.25, 4, 8)
    for k in range(K):
        x1_out[k] = xd[k + 1, :, 12:28, :]
    for k in range(PLANES):
        f1_out[k] = f1[k, :, 4:20, :]


def middle_kernel(own, on, off, x2_out, f2, chunk, xa, xb, inv, ratio, rs, gs, f3):
    even = lax.axis_index("gx") % 2 == 0

    def assemble(up, down):
        for k in range(PLANES):
            f2[k, :, 0:1, :] = jnp.zeros((2, 1, 128), F32)
            f2[k, :, 1:6, :] = up[k, :, 1:6, :]
            f2[k, :, 6:10, :] = own[k, :, 2:6, :]
            f2[k, :, 10:15, :] = down[k, :, 2:7, :]
            f2[k, :, 15:16, :] = jnp.zeros((2, 1, 128), F32)

    parity_copy(even, on, off, assemble)
    h = 0.25**2
    clear_edges(xa, 16)
    clear_edges(xb, 16)
    scales(f2, inv, ratio, h)
    first_sweep(xa, f2, inv, 16)
    second_sweep(xa, xb, f2, inv, 16, h)
    restrict(xb, f2, inv, ratio, rs, gs, f3, 16, h, 0, 8)
    for k in range(K):
        x2_out[k] = xb[k + 1, :, 8:24, :]
    rows = [f3[k, 0, 3:5, :] for k in range(PLANES)]
    rows.append(jnp.zeros((2, 128), F32))
    piece = jnp.concatenate(rows, axis=0)

    def fill(i, carry):
        chunk[i] = piece
        return carry

    lax.fori_loop(0, chunk.shape[0], fill, 0)


def add_copies(x, coarse, es, at_row, n, rows, first, count):
    chunks = coarse.shape[1]
    for k in range(K):
        for c in range(chunks):
            es[(k * chunks + c) * n : (k * chunks + c) * n + n, :] = coarse[k + 1, c, 8 + at_row : 8 + at_row + n, :]
    wide = exact_dot(es[...], copy_matrix(256))
    skip = (2 * n - rows) // 4
    used = rows // 2
    for k in range(K):
        for c in range(chunks):
            base = (k * chunks + c) * n + skip
            for half in range(2):
                fc = 2 * c + half - first
                if 0 <= fc < count:
                    e = wide[base : base + used, 128 * half : 128 * half + 128]
                    for p in range(2):
                        x[k + 1, fc, pl.ds(8 + p, used, stride=2), :] += e


def edge_kernel(plane, copy, edge):
    copy[...] = plane[...]
    first = lax.axis_index("gx") % PLANE < PLANE // 2

    @pl.when(first)
    def _():
        edge[...] = plane[PLANE - EXTRA : PLANE]

    @pl.when(jnp.logical_not(first))
    def _():
        edge[...] = plane[0:EXTRA]


def coarse_kernel(
    plane, beyond, before, after, x2_in, f2, x1_in, f1, x0_in, f0, guess, updated, new_defect,
    window, f3, xa, xb, inv3, ratio3, rs3, gs3, f4, ya, yb, inv4, es3, es2, xc, xd, inv2, es1, xe, xf, inv1, es0, xg, xh, inv0,
):
    gx = lax.axis_index("gx")
    tiles = lax.axis_size("gx")
    place = gx % PLANE
    above, below = EXTRA, EXTRA + 2 * PLANE

    window[above : above + PLANE] = before[...]
    window[above + PLANE : below] = plane[...]
    window[below : below + PLANE] = after[...]

    @pl.when(place < PLANE // 2)
    def _():
        window[0:EXTRA] = beyond[...]

    @pl.when(place >= PLANE // 2)
    def _():
        window[below + PLANE : below + PLANE + EXTRA] = beyond[...]

    for t in range(TILES):
        tile = gx - SIDE + t
        valid = jnp.logical_and(tile >= 0, tile < tiles)
        piece = jnp.where(valid, window[place + t], 0.0)
        for k in range(PLANES):
            f3[k, 0, 2 * t : 2 * t + 2, :] = piece[2 * k : 2 * k + 2]
    for k in range(PLANES):
        f3[k, 0, 2 * TILES : 48, :] = jnp.zeros((48 - 2 * TILES, 128), F32)
    h = 0.25**3
    clear_edges(xa, 48)
    clear_edges(xb, 48)
    scales(f3, inv3, ratio3, h)
    first_sweep(xa, f3, inv3, 48)
    second_sweep(xa, xb, f3, inv3, 48, h)
    restrict(xb, f3, inv3, ratio3, rs3, gs3, f4, 48, h, 0, 24)

    h = 0.25**4
    clear_edges(ya, 24)
    clear_edges(yb, 24)
    scales(f4, inv4, None, h)
    first_sweep(ya, f4, inv4, 24)
    second_sweep(ya, yb, f4, inv4, 24, h)
    for _ in range(3):
        sweep(yb, ya, f4, inv4, 24, h)
        sweep(ya, yb, f4, inv4, 24, h)

    h = 0.25**3
    for k in range(K):
        es3[24 * k : 24 * k + 24, :] = yb[k + 1, 0, 8:32, :]
    wide = exact_dot(es3[...], copy_matrix(128))
    for k in range(K):
        for p in range(2):
            xb[k + 1, 0, pl.ds(8 + p, 24, stride=2), :] += wide[24 * k : 24 * k + 24]
    sweep(xb, xa, f3, inv3, 48, h)
    sweep(xa, xb, f3, inv3, 48, h)

    h = 0.25**2
    clear_edges(xc, 16)
    clear_edges(xd, 16)
    scales(f2, inv2, None, h)
    for k in range(K):
        xc[k + 1, :, 8:24, :] = x2_in[k]
    add_copies(xc, xb, es2, 19, 8, 16, 0, 2)
    sweep(xc, xd, f2, inv2, 16, h)
    sweep(xd, xc, f2, inv2, 16, h)

    h = 0.25
    clear_edges(xe, 16)
    clear_edges(xf, 16)
    scales(f1, inv1, None, h)
    for k in range(K):
        xe[k + 1, :, 8:24, :] = x1_in[k]
    add_copies(xe, xc, es1, 4, 8, 16, 0, 4)
    sweep(xe, xf, f1, inv1, 16, h)
    sweep(xf, xe, f1, inv1, 16, h)

    clear_edges(xg, 24)
    clear_edges(xh, 24)
    scales(f0, inv0, None, 1.0)
    for k in range(K):
        xg[k + 1, :, 8:32, :] = x0_in[k]
    add_copies(xg, xe, es0, 0, 16, 24, 1, 6)
    sweep(xg, xh, f0, inv0, 24, 1.0)
    sweep(xh, xg, f0, inv0, 24, 1.0)

    for k in range(K):
        for c, (v, hs, vs) in enumerate(stencil(xg, k, 16, 12)):
            if 1 <= c <= 4:
                vc = f0[VC, c, 4:20, :]
                center = 4.0 + 2.0 * vc + f0[BT, c, 4:20, :]
                cols = slice(128 * (c - 1), 128 * c)
                new_defect[k, :, cols] = f0[k, c, 4:20, :] - center * v + hs + vc * vs
                updated[k, :, cols] = guess[k, :, cols] + v


def call(kernel, name, outs, scratch, *operands, space=pltpu.VMEM, mib=48):
    spec = pl.BlockSpec(memory_space=pltpu.VMEM)
    return pl.pallas_call(
        kernel,
        name=name,
        out_shape=[jax.ShapeDtypeStruct(s, F32) for s in outs],
        in_specs=[pl.BlockSpec(memory_space=space)] * len(operands),
        out_specs=[spec] * len(outs),
        scratch_shapes=[pltpu.VMEM(s, F32) if isinstance(s, tuple) else s for s in scratch],
        compiler_params=pltpu.CompilerParams(vmem_limit_bytes=mib * 1024 * 1024),
    )(*operands)


def field(chunks, rows):
    return (K + 2, chunks, rows + 16, 128)


def shards(right_side, guess, vertical, breaking):
    nx, ny = lax.axis_size("gx"), lax.axis_size("gy")
    chip = [(i, i ^ 1) for i in range(nx)]
    gap = [(i, i + 1) for i in range(1, nx - 1, 2)]
    gap = gap + [(b, a) for a, b in gap]

    to_inside, to_across = call(
        pack_kernel,
        "pack",
        [(Y_ROWS, 128), (Y_ROWS, 128)],
        [(K, 16, 512), (K, 16, 512), (16, 512), pltpu.VMEM((16, 512), jnp.int32), pltpu.SemaphoreType.DMA((4,))],
        right_side, guess, vertical, breaking,
        space=pltpu.HBM,
        mib=62,
    )
    inside = [(j, j ^ 1) for j in range(ny)]
    across = [(j, j + 1) for j in range(1, ny - 1, 2)]
    across = lax.ppermute(to_across, "gy", across + [(b, a) for a, b in across])
    inside = lax.ppermute(to_inside, "gy", inside)
    q, to_on, to_off = call(
        widen_kernel,
        "widen",
        [(PLANES + 2, 8, 16, 128), (7, X_ROWS, 128), (7, X_ROWS, 128)],
        [],
        right_side, guess, vertical, breaking, inside, across,
    )
    off = lax.ppermute(to_off, "gx", gap)
    on = lax.ppermute(to_on, "gx", chip)
    x0, f0, x1, f1, f2_own = call(
        fine_kernel,
        "fine",
        [(K, 6, 24, 128), (PLANES, 6, 24, 128), (K, 4, 16, 128), (PLANES, 4, 16, 128), (PLANES, 2, 8, 128)],
        [
            (PLANES, 8, 48, 128), field(8, 48), field(8, 48), (8, 48, 128), (8, 48, 128), (8, 64, 128), (K, 4 * 24, 256),
            (PLANES, 4, 24, 128), field(4, 24), field(4, 24), (4, 24, 128), (4, 24, 128), (4, 40, 128), (K, 2 * 8, 256),
        ],
        q, off, on,
    )
    off = lax.ppermute(f2_own, "gx", gap)
    on = lax.ppermute(f2_own, "gx", chip)
    x2, f2, chunk = call(
        middle_kernel,
        "middle",
        [(K, 2, 16, 128), (PLANES, 2, 16, 128), (PLANE, 24, 128)],
        [field(2, 16), field(2, 16), (2, 16, 128), (2, 16, 128), (2, 32, 128), (K, 8, 256), (PLANES, 1, 8, 128)],
        f2_own, on, off,
    )
    groups = [list(range(i, i + PLANE)) for i in range(0, nx, PLANE)]
    plane = lax.all_to_all(chunk, "gx", 0, 0, axis_index_groups=groups, tiled=True)
    plane, edge = call(edge_kernel, "edge", [(PLANE, 24, 128), (EXTRA, 24, 128)], [], plane)
    far = [(i, i + 2 * PLANE) for i in range(nx - 2 * PLANE) if i % PLANE < EXTRA]
    far += [(i, i - 2 * PLANE) for i in range(2 * PLANE, nx) if i % PLANE >= PLANE - EXTRA]
    beyond = lax.ppermute(edge, "gx", far)
    before = lax.ppermute(plane, "gx", [(i, i + PLANE) for i in range(nx - PLANE)])
    after = lax.ppermute(plane, "gx", [(i + PLANE, i) for i in range(nx - PLANE)])
    return tuple(
        call(
            coarse_kernel,
            "coarse",
            [(K, 16, 512), (K, 16, 512)],
            [
                (2 * EXTRA + 3 * PLANE, 24, 128),
                (PLANES, 1, 48, 128), field(1, 48), field(1, 48), (1, 48, 128), (1, 48, 128), (1, 64, 128), (K, 24, 128),
                (PLANES, 1, 24, 128), field(1, 24), field(1, 24), (1, 24, 128), (K * 24, 128),
                (K * 8, 128), field(2, 16), field(2, 16), (2, 16, 128),
                (K * 2 * 8, 128), field(4, 16), field(4, 16), (4, 16, 128),
                (K * 4 * 16, 128), field(6, 24), field(6, 24), (6, 24, 128),
            ],
            plane, beyond, before, after, x2, f2, x1, f1, x0, f0, guess,
        )
    )


def solution(mesh):
    in_specs = (P(None, "gx", "gy"), P(None, "gx", "gy"), P("gx", "gy"), P("gx", "gy"))
    out_specs = (P(None, "gx", "gy"), P(None, "gx", "gy"))
    return jax.shard_map(shards, mesh=mesh, in_specs=in_specs, out_specs=out_specs, check_vma=False)
```

```python
import jax
import jax.numpy as jnp
from jax import lax
from jax.experimental import pallas as pl
from jax.experimental.pallas import tpu as pltpu
from jax.sharding import PartitionSpec as P

K = 9
PLANES = K + 2
VC, BT = K, K + 1
TILES = 23
SIDE = TILES // 2
PLANE = 8
EXTRA = SIDE - PLANE
damping = 0.8
keep = 0.2
break_gain = 0.05
F32 = jnp.float32
BF16 = jnp.bfloat16

COLS_AT = 24 * PLANES
TOP_AT = COLS_AT + 16
BOTTOM_AT = TOP_AT + K
FAR_AT = BOTTOM_AT + K
Y_ROWS = FAR_AT + K + 5

SHORT_AT = 8 * PLANES
GUESS_AT = SHORT_AT + 5 * PLANES
X_ROWS = GUESS_AT + K


def lanes(rows):
    return lax.broadcasted_iota(jnp.int32, (rows, 128), 1)


def shifted(chunks):
    lane = lanes(chunks[0].shape[0])
    right = [pltpu.roll(v, 1, 1) for v in chunks]
    left = [pltpu.roll(v, 127, 1) for v in chunks]
    n = len(chunks)
    before = [jnp.where(lane == 0, right[c - 1], right[c]) if c else right[c] for c in range(n)]
    after = [jnp.where(lane == 127, left[c + 1], left[c]) if c < n - 1 else left[c] for c in range(n)]
    return before, after


def stencil(x, k, rows, at):
    count = x.shape[1]
    here = pl.ds(at, rows)
    v = [x[k + 1, c, here, :] for c in range(count)]
    before, after = shifted(v)
    out = []
    for c in range(count):
        hs = (x[k + 1, c, pl.ds(at - 1, rows), :] + x[k + 1, c, pl.ds(at + 1, rows), :]) + (before[c] + after[c])
        vs = x[k, c, here, :] + x[k + 2, c, here, :]
        out.append((v[c], hs, vs))
    return out


def clear_edges(x, rows):
    count, total = x.shape[1], x.shape[2]
    for k in (0, K + 1):
        x[k] = jnp.zeros((count, total, 128), F32)
    for k in range(1, K + 1):
        x[k, :, 0:8, :] = jnp.zeros((count, 8, 128), F32)
        x[k, :, 8 + rows : total, :] = jnp.zeros((count, total - 8 - rows, 128), F32)


def scales(f, inv, ratio, h):
    for c in range(f.shape[1]):
        vc = f[VC, c]
        center = 4.0 * h + 2.0 * vc + f[BT, c]
        inv[c] = jnp.where(vc > 0.0, damping / center, 0.0)
        if ratio is not None:
            ratio[c] = center * (1.0 / damping)


def first_sweep(x, f, inv, rows):
    for k in range(K):
        for c in range(f.shape[1]):
            x[k + 1, c, pl.ds(8, rows), :] = inv[c] * f[k, c]


def times(h, value):
    return value if h == 1.0 else h * value


def second_sweep(x, y, f, inv, rows, h):
    for k in range(K):
        for c, (v, hs, vs) in enumerate(stencil(x, k, rows, 8)):
            y[k + 1, c, pl.ds(8, rows), :] = (1.0 + keep) * v + inv[c] * (times(h, hs) + f[VC, c] * vs)


def sweep(x, y, f, inv, rows, h):
    for k in range(K):
        for c, (v, hs, vs) in enumerate(stencil(x, k, rows, 8)):
            y[k + 1, c, pl.ds(8, rows), :] = keep * v + inv[c] * (f[k, c] + times(h, hs) + f[VC, c] * vs)


def pair_matrix(inputs):
    i = lax.broadcasted_iota(jnp.int32, (inputs, 128), 0)
    j = lax.broadcasted_iota(jnp.int32, (inputs, 128), 1)
    return jnp.where((i == 2 * j) | (i == 2 * j + 1), 0.25, 0.0).astype(BF16)


def fold_matrix(inputs):
    i = lax.broadcasted_iota(jnp.int32, (inputs, 128), 0)
    d = i - 2 * lax.broadcasted_iota(jnp.int32, (inputs, 128), 1)
    inner = jnp.where((d == 0) | (d == 1), 0.375, 0.0)
    return jnp.where((d == -1) | (d == 2), 0.125, inner).astype(BF16)


def copy_matrix(outputs):
    i = lax.broadcasted_iota(jnp.int32, (128, outputs), 0)
    j = lax.broadcasted_iota(jnp.int32, (128, outputs), 1)
    return jnp.where((j == 2 * i) | (j == 2 * i + 1), 1.0, 0.0).astype(BF16)


def exact_dot(values, matrix, parts=3):
    total = None
    for _ in range(parts):
        part = values.astype(BF16)
        values = values - part.astype(F32)
        product = jnp.dot(part, matrix, preferred_element_type=F32)
        total = product if total is None else total + product
    return total


def restrict(x, f, inv, ratio, rs, gs, coarse, rows, h, base, n):
    count = f.shape[1]
    pairs = max(count // 2, 1)
    width = gs.shape[-1]
    lane = lanes(n)
    rs[:, 0:8, :] = jnp.zeros((count, 8, 128), F32)
    rs[:, 8 + rows : 16 + rows, :] = jnp.zeros((count, 8, 128), F32)

    def part(slot, c):
        return gs[slot, (c // 2) * n : (c // 2) * n + n, 128 * (c % 2) : 128 * (c % 2) + 128]

    def put(slot, c, value):
        gs[slot, (c // 2) * n : (c // 2) * n + n, 128 * (c % 2) : 128 * (c % 2) + 128] = value

    def residual(k, slot):
        for c, (v, hs, vs) in enumerate(stencil(x, k, rows, 8)):
            around = inv[c] * (f[k, c] + times(h, hs) + f[VC, c] * vs)
            rs[c, 8 : 8 + rows, :] = ratio[c] * (around - damping * v)
        for c in range(count):

            def pick(start):
                return rs[c, pl.ds(8 + base + start, n, stride=2), :]

            put(slot, c, (pick(-1) + 3.0 * (pick(0) + pick(1)) + pick(2)) * 0.125)

    def emit(k, slot, values):
        for j in range(pairs):
            value = values[j * n : j * n + n]
            if j > 0:
                value = value + jnp.where(lane == 0, 0.125 * pltpu.roll(part(slot, 2 * j - 1), 1, 1), 0.0)
            if j < pairs - 1:
                value = value + jnp.where(lane == 127, 0.125 * pltpu.roll(part(slot, 2 * j + 2), 127, 1), 0.0)
            coarse[k, j] = value

    matrix = fold_matrix(width)
    for k in range(K):
        residual(k, k)
    size = pairs * n
    values = exact_dot(gs[...].reshape(K * size, width), matrix, 2)
    for k in range(K):
        emit(k, k, values[k * size : k * size + size])
    for slot, k in enumerate((VC, BT)):
        for c in range(count):
            put(slot, c, f[k, c, pl.ds(base, n, stride=2), :] + f[k, c, pl.ds(base + 1, n, stride=2), :])
    values = exact_dot(gs[0:2].reshape(2 * pairs * n, width), pair_matrix(width))
    for slot, k in enumerate((VC, BT)):
        for j in range(pairs):
            at = (slot * pairs + j) * n
            coarse[k, j] = values[at : at + n]


def parity_copy(even, on, off, assemble):
    @pl.when(even)
    def _():
        assemble(off, on)

    @pl.when(jnp.logical_not(even))
    def _():
        assemble(on, off)


def own_defect(right_side, guess, vc, bt, k, left, right):
    v = guess[k]
    row = lax.broadcasted_iota(jnp.int32, v.shape, 0)
    col = lax.broadcasted_iota(jnp.int32, v.shape, 1)
    hs = jnp.where(row > 0, pltpu.roll(v, 1, 0), 0.0) + jnp.where(row < 15, pltpu.roll(v, 15, 0), 0.0)
    hs = hs + jnp.where(col > 0, pltpu.roll(v, 1, 1), left) + jnp.where(col < 511, pltpu.roll(v, 511, 1), right)
    vs = guess[1] if k == 0 else guess[K - 2] if k == K - 1 else guess[k - 1] + guess[k + 1]
    return right_side[k] - (4.0 + 2.0 * vc + bt) * v + hs + vc * vs


def pack_kernel(rs_in, g_in, vc_in, br_in, to_inside, to_across, right_side, guess, vertical, breaking, sems):
    pairs = ((vc_in, vertical), (br_in, breaking), (g_in, guess), (rs_in, right_side))
    copies = [pltpu.make_async_copy(a, b, sems.at[i]) for i, (a, b) in enumerate(pairs)]
    for copy in copies:
        copy.start()
    for copy in copies:
        copy.wait()
    lane = lanes(16)
    lane8 = lanes(8)
    vc = vertical[...]
    bt = break_gain * breaking[...].astype(F32)

    def pack_all(to_right, to_left):
        def pack(plane, field):
            near, far = field[:, 0:128], field[:, 128:256]
            to_left[24 * plane : 24 * plane + 16, :] = near
            to_left[24 * plane + 16 : 24 * plane + 24, :] = jnp.where(
                lane8 < 64, far[0:8], pltpu.roll(far[8:16], 64, 1)
            )
            near, far = field[:, 384:512], field[:, 256:384]
            to_right[24 * plane : 24 * plane + 16, :] = near
            to_right[24 * plane + 16 : 24 * plane + 24, :] = jnp.where(
                lane8 >= 64, far[0:8], pltpu.roll(far[8:16], 64, 1)
            )

        first = jnp.zeros((16, 128), F32)
        last = jnp.zeros((16, 128), F32)
        to_left[TOP_AT:Y_ROWS, :] = jnp.zeros((Y_ROWS - TOP_AT, 128), F32)
        to_right[TOP_AT:Y_ROWS, :] = jnp.zeros((Y_ROWS - TOP_AT, 128), F32)
        lane1 = lanes(1)
        for k in range(K):
            v = guess[k]
            f = own_defect(right_side, guess, vc, bt, k, 0.0, 0.0)
            pack(k, f)
            first = jnp.where(lane == k, jnp.broadcast_to(v[:, 0:1], (16, 128)), first)
            last = jnp.where(lane == k, jnp.broadcast_to(v[:, 511:512], (16, 128)), last)
            top, bottom = v[0:1], v[15:16]
            to_left[TOP_AT + k : TOP_AT + k + 1, :] = top[:, 0:128]
            to_left[BOTTOM_AT + k : BOTTOM_AT + k + 1, :] = bottom[:, 0:128]
            to_left[FAR_AT + k : FAR_AT + k + 1, :] = jnp.where(
                lane1 < 64, top[:, 128:256], pltpu.roll(bottom[:, 128:256], 64, 1)
            )
            to_right[TOP_AT + k : TOP_AT + k + 1, :] = top[:, 384:512]
            to_right[BOTTOM_AT + k : BOTTOM_AT + k + 1, :] = bottom[:, 384:512]
            to_right[FAR_AT + k : FAR_AT + k + 1, :] = jnp.where(
                lane1 >= 64, top[:, 256:384], pltpu.roll(bottom[:, 256:384], 64, 1)
            )
        pack(VC, vc)
        pack(BT, bt)
        to_left[COLS_AT : COLS_AT + 16, :] = first
        to_right[COLS_AT : COLS_AT + 16, :] = last

    parity_copy(lax.axis_index("gy") % 2 == 0, to_inside, to_across, lambda left, right: pack_all(right, left))


def widen_kernel(right_side, guess, vertical, breaking, inside, across, q, to_on, to_off):
    lane = lanes(16)

    def assemble(from_left, from_right):
        lane = lanes(16)
        lane8 = lanes(8)
        lane1 = lanes(1)
        left_cols = from_left[COLS_AT : COLS_AT + 16, :]
        right_cols = from_right[COLS_AT : COLS_AT + 16, :]
        vc = vertical[...]
        bt = break_gain * breaking[...].astype(F32)
        for k in range(PLANES):
            far = from_left[24 * k + 16 : 24 * k + 24, :]
            q[k, 0, 0:8, :] = jnp.where(lane8 >= 64, far, 0.0)
            q[k, 0, 8:16, :] = jnp.where(lane8 >= 64, pltpu.roll(far, 64, 1), 0.0)
            far = from_right[24 * k + 16 : 24 * k + 24, :]
            q[k, 7, 0:8, :] = jnp.where(lane8 < 64, far, 0.0)
            q[k, 7, 8:16, :] = jnp.where(lane8 < 64, pltpu.roll(far, 64, 1), 0.0)
            near_left = from_left[24 * k : 24 * k + 16, :]
            near_right = from_right[24 * k : 24 * k + 16, :]
            if k < K:
                v = guess[k]
                first = jnp.broadcast_to(v[:, 0:1], (16, 128))
                last = jnp.broadcast_to(v[:, 511:512], (16, 128))
                q[k, 1] = near_left + jnp.where(lane == 127, first, 0.0)
                q[k, 6] = near_right + jnp.where(lane == 0, last, 0.0)
                own = own_defect(right_side, guess, vc, bt, k, left_cols[:, k : k + 1], right_cols[:, k : k + 1])
            else:
                q[k, 1] = near_left
                q[k, 6] = near_right
                own = vc if k == VC else bt
            for c in range(4):
                q[k, 2 + c] = own[:, 128 * c : 128 * c + 128]
        for plane, row, near_at in ((PLANES, 0, TOP_AT), (PLANES + 1, 15, BOTTOM_AT)):
            for c in range(8):
                q[plane, c] = jnp.zeros((16, 128), F32)
            for k in range(K):
                at = slice(k, k + 1)
                v = guess[k, row : row + 1, :]
                for c in range(4):
                    q[plane, 2 + c, at, :] = v[:, 128 * c : 128 * c + 128]
                q[plane, 1, at, :] = from_left[near_at + k : near_at + k + 1, :]
                q[plane, 6, at, :] = from_right[near_at + k : near_at + k + 1, :]
                far_left = from_left[FAR_AT + k : FAR_AT + k + 1, :]
                far_right = from_right[FAR_AT + k : FAR_AT + k + 1, :]
                if plane == PLANES + 1:
                    far_left = pltpu.roll(far_left, 64, 1)
                    far_right = pltpu.roll(far_right, 64, 1)
                q[plane, 0, at, :] = jnp.where(lane1 >= 64, far_left, 0.0)
                q[plane, 7, at, :] = jnp.where(lane1 < 64, far_right, 0.0)

    parity_copy(lax.axis_index("gy") % 2 == 0, inside, across, assemble)

    def fill(buffer, long, short, plane):
        for c in range(7):
            for k in range(PLANES):
                piece = jnp.where(lane < 64, q[k, 7], q[k, 0]) if c == 0 else q[k, c]
                buffer[c, 8 * k : 8 * k + 8, :] = piece[long : long + 8]
                buffer[c, SHORT_AT + 5 * k : SHORT_AT + 5 * k + 5, :] = piece[short : short + 5]
            piece = jnp.where(lane < 64, q[plane, 7], q[plane, 0]) if c == 0 else q[plane, c]
            buffer[c, GUESS_AT : GUESS_AT + K, :] = piece[0:K]

    def fill_both(to_up, to_down):
        fill(to_up, 0, 8, PLANES)
        fill(to_down, 8, 3, PLANES + 1)

    parity_copy(lax.axis_index("gx") % 2 == 0, to_on, to_off, fill_both)


def fine_kernel(q, off, on, x0_out, f0_out, x1_out, f1_out, f2_out, f, xa, xb, inv, ratio, rs, gs, f1, xc, xd, inv1, ratio1, rs1, gs1):
    even = lax.axis_index("gx") % 2 == 0

    def assemble(up, down):
        lane = lanes(8)

        def piece(buffer, c, at, n):
            value = buffer[min(c % 7, c), at : at + n, :]
            if c == 0:
                return jnp.where(lane[0:n] >= 64, value, 0.0)
            return jnp.where(lane[0:n] < 64, value, 0.0) if c == 7 else value

        for c in range(8):
            for k in range(PLANES):
                short = SHORT_AT + 5 * k
                f[k, c, 0:3, :] = jnp.zeros((3, 128), F32)
                f[k, c, 3:8, :] = piece(up, c, short, 5)
                f[k, c, 8:16, :] = piece(up, c, 8 * k, 8)
                f[k, c, 16:32, :] = q[k, c]
                f[k, c, 32:40, :] = piece(down, c, 8 * k, 8)
                f[k, c, 40:45, :] = piece(down, c, short, 5)
                f[k, c, 45:48, :] = jnp.zeros((3, 128), F32)
            for k in range(K):
                row = slice(k, k + 1)
                f[k, c, 15:16, :] += q[PLANES, c, row, :]
                f[k, c, 16:17, :] += piece(up, c, GUESS_AT + k, 1)
                f[k, c, 31:32, :] += piece(down, c, GUESS_AT + k, 1)
                f[k, c, 32:33, :] += q[PLANES + 1, c, row, :]

    parity_copy(even, on, off, assemble)
    clear_edges(xa, 48)
    clear_edges(xb, 48)
    scales(f, inv, ratio, 1.0)
    first_sweep(xa, f, inv, 48)
    second_sweep(xa, xb, f, inv, 48, 1.0)
    restrict(xb, f, inv, ratio, rs, gs, f1, 48, 1.0, 0, 24)
    for k in range(K):
        x0_out[k] = xb[k + 1, 1:7, 20:44, :]
    for k in range(PLANES):
        f0_out[k] = f[k, 1:7, 12:36, :]

    clear_edges(xc, 24)
    clear_edges(xd, 24)
    scales(f1, inv1, ratio1, 0.25)
    first_sweep(xc, f1, inv1, 24)
    second_sweep(xc, xd, f1, inv1, 24, 0.25)
    restrict(xd, f1, inv1, ratio1, rs1, gs1, f2_out, 24, 0.25, 4, 8)
    for k in range(K):
        x1_out[k] = xd[k + 1, :, 12:28, :]
    for k in range(PLANES):
        f1_out[k] = f1[k, :, 4:20, :]


def middle_kernel(own, on, off, x2_out, f2, chunk, xa, xb, inv, ratio, rs, gs, f3):
    even = lax.axis_index("gx") % 2 == 0

    def assemble(up, down):
        for k in range(PLANES):
            f2[k, :, 0:1, :] = jnp.zeros((2, 1, 128), F32)
            f2[k, :, 1:6, :] = up[k, :, 1:6, :]
            f2[k, :, 6:10, :] = own[k, :, 2:6, :]
            f2[k, :, 10:15, :] = down[k, :, 2:7, :]
            f2[k, :, 15:16, :] = jnp.zeros((2, 1, 128), F32)

    parity_copy(even, on, off, assemble)
    h = 0.25**2
    clear_edges(xa, 16)
    clear_edges(xb, 16)
    scales(f2, inv, ratio, h)
    first_sweep(xa, f2, inv, 16)
    second_sweep(xa, xb, f2, inv, 16, h)
    restrict(xb, f2, inv, ratio, rs, gs, f3, 16, h, 0, 8)
    for k in range(K):
        x2_out[k] = xb[k + 1, :, 8:24, :]
    rows = [f3[k, 0, 3:5, :] for k in range(PLANES)]
    rows.append(jnp.zeros((2, 128), F32))
    piece = jnp.concatenate(rows, axis=0)

    def fill(i, carry):
        chunk[i] = piece
        return carry

    lax.fori_loop(0, chunk.shape[0], fill, 0)


def add_copies(x, coarse, es, at_row, n, rows, first, count):
    chunks = coarse.shape[1]
    for k in range(K):
        for c in range(chunks):
            es[(k * chunks + c) * n : (k * chunks + c) * n + n, :] = coarse[k + 1, c, 8 + at_row : 8 + at_row + n, :]
    wide = exact_dot(es[...], copy_matrix(256))
    skip = (2 * n - rows) // 4
    used = rows // 2
    for k in range(K):
        for c in range(chunks):
            base = (k * chunks + c) * n + skip
            for half in range(2):
                fc = 2 * c + half - first
                if 0 <= fc < count:
                    e = wide[base : base + used, 128 * half : 128 * half + 128]
                    for p in range(2):
                        x[k + 1, fc, pl.ds(8 + p, used, stride=2), :] += e


def edge_kernel(plane, copy, edge):
    copy[...] = plane[...]
    first = lax.axis_index("gx") % PLANE < PLANE // 2

    @pl.when(first)
    def _():
        edge[...] = plane[PLANE - EXTRA : PLANE]

    @pl.when(jnp.logical_not(first))
    def _():
        edge[...] = plane[0:EXTRA]


def coarse_kernel(
    plane, beyond, before, after, x2_in, f2, x1_in, f1, x0_in, f0, guess, updated, new_defect,
    window, f3, xa, xb, inv3, ratio3, rs3, gs3, f4, ya, yb, inv4, es3, es2, xc, xd, inv2, es1, xe, xf, inv1, es0, xg, xh, inv0,
):
    gx = lax.axis_index("gx")
    tiles = lax.axis_size("gx")
    place = gx % PLANE
    above, below = EXTRA, EXTRA + 2 * PLANE

    window[above : above + PLANE] = before[...]
    window[above + PLANE : below] = plane[...]
    window[below : below + PLANE] = after[...]

    @pl.when(place < PLANE // 2)
    def _():
        window[0:EXTRA] = beyond[...]

    @pl.when(place >= PLANE // 2)
    def _():
        window[below + PLANE : below + PLANE + EXTRA] = beyond[...]

    for t in range(TILES):
        tile = gx - SIDE + t
        valid = jnp.logical_and(tile >= 0, tile < tiles)
        piece = jnp.where(valid, window[place + t], 0.0)
        for k in range(PLANES):
            f3[k, 0, 2 * t : 2 * t + 2, :] = piece[2 * k : 2 * k + 2]
    for k in range(PLANES):
        f3[k, 0, 2 * TILES : 48, :] = jnp.zeros((48 - 2 * TILES, 128), F32)
    h = 0.25**3
    clear_edges(xa, 48)
    clear_edges(xb, 48)
    scales(f3, inv3, ratio3, h)
    first_sweep(xa, f3, inv3, 48)
    second_sweep(xa, xb, f3, inv3, 48, h)
    restrict(xb, f3, inv3, ratio3, rs3, gs3, f4, 48, h, 0, 24)

    h = 0.25**4
    clear_edges(ya, 24)
    clear_edges(yb, 24)
    scales(f4, inv4, None, h)
    first_sweep(ya, f4, inv4, 24)
    second_sweep(ya, yb, f4, inv4, 24, h)
    for _ in range(3):
        sweep(yb, ya, f4, inv4, 24, h)
        sweep(ya, yb, f4, inv4, 24, h)

    h = 0.25**3
    for k in range(K):
        es3[24 * k : 24 * k + 24, :] = yb[k + 1, 0, 8:32, :]
    wide = exact_dot(es3[...], copy_matrix(128))
    for k in range(K):
        for p in range(2):
            xb[k + 1, 0, pl.ds(8 + p, 24, stride=2), :] += wide[24 * k : 24 * k + 24]
    sweep(xb, xa, f3, inv3, 48, h)
    sweep(xa, xb, f3, inv3, 48, h)

    h = 0.25**2
    clear_edges(xc, 16)
    clear_edges(xd, 16)
    scales(f2, inv2, None, h)
    for k in range(K):
        xc[k + 1, :, 8:24, :] = x2_in[k]
    add_copies(xc, xb, es2, 19, 8, 16, 0, 2)
    sweep(xc, xd, f2, inv2, 16, h)
    sweep(xd, xc, f2, inv2, 16, h)

    h = 0.25
    clear_edges(xe, 16)
    clear_edges(xf, 16)
    scales(f1, inv1, None, h)
    for k in range(K):
        xe[k + 1, :, 8:24, :] = x1_in[k]
    add_copies(xe, xc, es1, 4, 8, 16, 0, 4)
    sweep(xe, xf, f1, inv1, 16, h)
    sweep(xf, xe, f1, inv1, 16, h)

    clear_edges(xg, 24)
    clear_edges(xh, 24)
    scales(f0, inv0, None, 1.0)
    for k in range(K):
        xg[k + 1, :, 8:32, :] = x0_in[k]
    add_copies(xg, xe, es0, 0, 16, 24, 1, 6)
    sweep(xg, xh, f0, inv0, 24, 1.0)
    sweep(xh, xg, f0, inv0, 24, 1.0)

    for k in range(K):
        for c, (v, hs, vs) in enumerate(stencil(xg, k, 16, 12)):
            if 1 <= c <= 4:
                vc = f0[VC, c, 4:20, :]
                center = 4.0 + 2.0 * vc + f0[BT, c, 4:20, :]
                cols = slice(128 * (c - 1), 128 * c)
                new_defect[k, :, cols] = f0[k, c, 4:20, :] - center * v + hs + vc * vs
                updated[k, :, cols] = guess[k, :, cols] + v


def call(kernel, name, outs, scratch, *operands, space=pltpu.VMEM, mib=48):
    spec = pl.BlockSpec(memory_space=pltpu.VMEM)
    return pl.pallas_call(
        kernel,
        name=name,
        out_shape=[jax.ShapeDtypeStruct(s, F32) for s in outs],
        in_specs=[pl.BlockSpec(memory_space=space)] * len(operands),
        out_specs=[spec] * len(outs),
        scratch_shapes=[pltpu.VMEM(s, F32) if isinstance(s, tuple) else s for s in scratch],
        compiler_params=pltpu.CompilerParams(vmem_limit_bytes=mib * 1024 * 1024),
    )(*operands)


def field(chunks, rows):
    return (K + 2, chunks, rows + 16, 128)


def shards(right_side, guess, vertical, breaking):
    nx, ny = lax.axis_size("gx"), lax.axis_size("gy")
    chip = [(i, i ^ 1) for i in range(nx)]
    gap = [(i, i + 1) for i in range(1, nx - 1, 2)]
    gap = gap + [(b, a) for a, b in gap]

    to_inside, to_across = call(
        pack_kernel,
        "pack",
        [(Y_ROWS, 128), (Y_ROWS, 128)],
        [(K, 16, 512), (K, 16, 512), (16, 512), pltpu.VMEM((16, 512), jnp.int32), pltpu.SemaphoreType.DMA((4,))],
        right_side, guess, vertical, breaking,
        space=pltpu.HBM,
        mib=62,
    )
    inside = [(j, j ^ 1) for j in range(ny)]
    across = [(j, j + 1) for j in range(1, ny - 1, 2)]
    across = lax.ppermute(to_across, "gy", across + [(b, a) for a, b in across])
    inside = lax.ppermute(to_inside, "gy", inside)
    q, to_on, to_off = call(
        widen_kernel,
        "widen",
        [(PLANES + 2, 8, 16, 128), (7, X_ROWS, 128), (7, X_ROWS, 128)],
        [],
        right_side, guess, vertical, breaking, inside, across,
    )
    off = lax.ppermute(to_off, "gx", gap)
    on = lax.ppermute(to_on, "gx", chip)
    x0, f0, x1, f1, f2_own = call(
        fine_kernel,
        "fine",
        [(K, 6, 24, 128), (PLANES, 6, 24, 128), (K, 4, 16, 128), (PLANES, 4, 16, 128), (PLANES, 2, 8, 128)],
        [
            (PLANES, 8, 48, 128), field(8, 48), field(8, 48), (8, 48, 128), (8, 48, 128), (8, 64, 128), (K, 4 * 24, 256),
            (PLANES, 4, 24, 128), field(4, 24), field(4, 24), (4, 24, 128), (4, 24, 128), (4, 40, 128), (K, 2 * 8, 256),
        ],
        q, off, on,
    )
    off = lax.ppermute(f2_own, "gx", gap)
    on = lax.ppermute(f2_own, "gx", chip)
    x2, f2, chunk = call(
        middle_kernel,
        "middle",
        [(K, 2, 16, 128), (PLANES, 2, 16, 128), (PLANE, 24, 128)],
        [field(2, 16), field(2, 16), (2, 16, 128), (2, 16, 128), (2, 32, 128), (K, 8, 256), (PLANES, 1, 8, 128)],
        f2_own, on, off,
    )
    groups = [list(range(i, i + PLANE)) for i in range(0, nx, PLANE)]
    plane = lax.all_to_all(chunk, "gx", 0, 0, axis_index_groups=groups, tiled=True)
    plane, edge = call(edge_kernel, "edge", [(PLANE, 24, 128), (EXTRA, 24, 128)], [], plane)
    far = [(i, i + 2 * PLANE) for i in range(nx - 2 * PLANE) if i % PLANE < EXTRA]
    far += [(i, i - 2 * PLANE) for i in range(2 * PLANE, nx) if i % PLANE >= PLANE - EXTRA]
    beyond = lax.ppermute(edge, "gx", far)
    before = lax.ppermute(plane, "gx", [(i, i + PLANE) for i in range(nx - PLANE)])
    after = lax.ppermute(plane, "gx", [(i + PLANE, i) for i in range(nx - PLANE)])
    return tuple(
        call(
            coarse_kernel,
            "coarse",
            [(K, 16, 512), (K, 16, 512)],
            [
                (2 * EXTRA + 3 * PLANE, 24, 128),
                (PLANES, 1, 48, 128), field(1, 48), field(1, 48), (1, 48, 128), (1, 48, 128), (1, 64, 128), (K, 24, 128),
                (PLANES, 1, 24, 128), field(1, 24), field(1, 24), (1, 24, 128), (K * 24, 128),
                (K * 8, 128), field(2, 16), field(2, 16), (2, 16, 128),
                (K * 2 * 8, 128), field(4, 16), field(4, 16), (4, 16, 128),
                (K * 4 * 16, 128), field(6, 24), field(6, 24), (6, 24, 128),
            ],
            plane, beyond, before, after, x2, f2, x1, f1, x0, f0, guess,
        )
    )


def solution(mesh):
    in_specs = (P(None, "gx", "gy"), P(None, "gx", "gy"), P("gx", "gy"), P("gx", "gy"))
    out_specs = (P(None, "gx", "gy"), P(None, "gx", "gy"))
    return jax.shard_map(shards, mesh=mesh, in_specs=in_specs, out_specs=out_specs, check_vma=False)
```
